256 devices in a mesh: dp: 16 (over y, z_lo, core), blk: 16 (over z_hi, x).
Axes of the slice: x: 4, y: 4, z: 8 (z_hi: 4, z_lo: 2; z = z_hi * 2 + z_lo), core: 2. Of those that a mesh axis runs over, the one named last changes fastest.
Arguments:
- q_long: bfloat16 [16, 2048, 1024], P('dp', 'blk'), may hold values from -4.5 to 4.5
- k_long: bfloat16 [16, 2048, 1024], P('dp', 'blk'), may hold values from -4.5 to 4.5
- v_long: bfloat16 [16, 2048, 1024], P('dp', 'blk'), may hold values from -6 to 6
- out_long: bfloat16 [16, 2048, 1024], P('dp', 'blk'), may hold values from -6 to 6
- grad_long: bfloat16 [16, 2048, 1024], P('dp', 'blk'), may hold values from -6 to 6
- cycle_group: int32 [16, 16], P('dp'), may hold values from 0 to 15, as said below
- gap_long: int32 [16, 2048], P('dp'), may hold values from 0 to 31
- q_short: bfloat16 [65536, 1024], P(('dp', 'blk')), may hold values from -4.5 to 4.5
- k_short: bfloat16 [65536, 1024], P(('dp', 'blk')), may hold values from -4.5 to 4.5
- v_short: bfloat16 [65536, 1024], P(('dp', 'blk')), may hold values from -6 to 6
- out_short: bfloat16 [65536, 1024], P(('dp', 'blk')), may hold values from -6 to 6
- grad_short: bfloat16 [65536, 1024], P(('dp', 'blk')), may hold values from -6 to 6
- short_lengths: int32 [512], P(('dp', 'blk')), may hold values from 1 to 128
- gap_short: int32 [65536], P(('dp', 'blk')), may hold values from 0 to 31
- bias_table: float32 [8, 32], replicated, may hold values from -4 to 4
Outputs:
- grad_q_long: bfloat16 [16, 2048, 1024], P('dp', 'blk')
- grad_k_long: bfloat16 [16, 2048, 1024], P('dp', 'blk')
- grad_v_long: bfloat16 [16, 2048, 1024], P('dp', 'blk')
- grad_q_short: bfloat16 [65536, 1024], P(('dp', 'blk'))
- grad_k_short: bfloat16 [65536, 1024], P(('dp', 'blk'))
- grad_v_short: bfloat16 [65536, 1024], P(('dp', 'blk'))
- grad_bias: float32 [8, 32], replicated
The draws below stay inside these ranges and needn't reach their ends.
Inputs may be any that keep to these rules, and one draw needn't show every extreme that they name: `cycle_group`: values never fall along a row; shards with one value form one history, and the value is the index of that history's first shard.
All inputs are finite; a program needn't handle non-finite values.
Results may differ from the reference program's by a relative error of at most 0.0049.
Values may be sent and summed in bfloat16 or wider, within the bound.
A program may use at most 64 MiB of HBM per device.

```python
import jax
import jax.numpy as jnp
from jax import lax

D = 1024
H = 8
HD = 128
NBK = 32
WIN = 4
SBLK = 128
S_DEV = 128
SEQS = 16
L = 2048
NSEG = 512
SHORT = 65536
N_BLK = 16


def paired(key, shape, strength, salt):
    key = jax.random.fold_in(key, salt)
    key_q, key_k, key_sign, key_amp = jax.random.split(key, 4)
    base_q = jnp.clip(jax.random.normal(key_q, shape, jnp.float32), -4.5, 4.5)
    base_k = jnp.clip(jax.random.normal(key_k, shape, jnp.float32), -4.5, 4.5)
    count = shape[-2]
    position = jnp.arange(count, dtype=jnp.int32).reshape((count, 1))
    marked = position % 97 == 7
    marked = jnp.logical_and(jnp.broadcast_to(marked, shape[:-1] + (1,)), strength > 0.0)
    sign = jnp.where(jax.random.normal(key_sign, shape, jnp.float32) >= 0.0, 1.0, -1.0)
    amp = strength * jax.random.uniform(key_amp, shape[:-1] + (1,), jnp.float32, 0.5, 1.5)
    line = amp * sign
    beside = jnp.roll((amp - 0.06) * sign, -1, axis=-2)
    marked_next = jnp.roll(marked, -1, axis=-2)
    query = jnp.where(marked, line, base_q)
    keys = jnp.where(marked, line, jnp.where(marked_next, beside, base_k))
    return (query, keys)


def draw_q_long(key, part):
    strength = 0.0
    return paired(key, (SEQS, L, D), strength, 1)[0].astype(jnp.bfloat16)


def draw_k_long(key, part):
    strength = 0.0
    return paired(key, (SEQS, L, D), strength, 1)[1].astype(jnp.bfloat16)


def draw_q_short(key, part):
    strength = 0.0
    return paired(key, (SHORT, D), strength, 2)[0].astype(jnp.bfloat16)


def draw_k_short(key, part):
    strength = 0.0
    return paired(key, (SHORT, D), strength, 2)[1].astype(jnp.bfloat16)


def draw_cycle_group(key, part):
    key = jax.random.fold_in(key, 11)
    marks = jax.random.randint(key, (SEQS, N_BLK), 0, 4) == 0
    index = jnp.broadcast_to(jnp.arange(N_BLK, dtype=jnp.int32)[None, :], (SEQS, N_BLK))
    first_row = jnp.arange(SEQS, dtype=jnp.int32)[:, None] == 0
    forced = (index == 0) | (index == N_BLK - 1) & first_row
    starts = marks | forced
    return lax.cummax(jnp.where(starts, index, 0), axis=1)


def place_ends(drawn, stream_key, least, largest):
    longest = drawn.shape.index(max(drawn.shape))
    spots = []
    for shift in (0, 1):
        where = [jax.random.randint(jax.random.fold_in(stream_key, axis), (), 0, length) for axis, length in enumerate(drawn.shape)]
        where[longest] = (where[longest] + shift) % drawn.shape[longest]
        spots.append(tuple(where))
    return drawn.at[spots[0]].set(least).at[spots[1]].set(largest)


def block_scale(key, dims, shards, low, largest):
    def one(axis_at, shards_of):
        steps = jax.random.uniform(jax.random.fold_in(jax.random.fold_in(key, 6), axis_at), (shards_of,), jnp.float32, low / len(shards), largest / len(shards))
        return jnp.repeat(jnp.exp(steps), dims[axis_at] // shards_of).reshape((-1,) + (1,) * (len(dims) - axis_at - 1))

    factor_of = one(*shards[0])
    for cut in shards[1:]:
        factor_of = factor_of * one(*cut)
    return factor_of


def noise(rng, shape, spread, most, cuts=(), kind=jnp.bfloat16):
    loudness = block_scale(rng, shape, cuts, -0.22, 0.18) if cuts else 1.0
    values = jax.random.normal(rng, shape, jnp.float32) * spread * loudness
    return jnp.minimum(jnp.maximum(values, -most), most).astype(kind)


def setup_inputs(seed: int = 0) -> dict:
    splits = jax.random.split(jax.random.key(seed), 16)
    q_long = draw_q_long(jax.random.fold_in(splits[15], 71), 0)
    k_long = draw_k_long(jax.random.fold_in(splits[15], 71), 0)
    v_long = noise(splits[2], (SEQS, L, D), 1.0, 6.0, ((0, 16), (1, 16)))
    out_long = noise(splits[3], (SEQS, L, D), 1.0, 6.0, ((0, 16), (1, 16)))
    grad_long = noise(splits[4], (SEQS, L, D), 1.0, 6.0, ((0, 16), (1, 16)))
    cycle_group = draw_cycle_group(jax.random.fold_in(splits[15], 71), 0)
    gap_long = place_ends(jax.random.randint(splits[6], (SEQS, L), 0, NBK), jax.random.fold_in(splits[6], 1), 0, NBK - 1).astype(jnp.int32)
    q_short = draw_q_short(jax.random.fold_in(splits[15], 71), 0)
    k_short = draw_k_short(jax.random.fold_in(splits[15], 71), 0)
    v_short = noise(splits[9], (SHORT, D), 1.0, 6.0, ((0, 256),))
    out_short = noise(splits[10], (SHORT, D), 1.0, 6.0, ((0, 256),))
    grad_short = noise(splits[11], (SHORT, D), 1.0, 6.0, ((0, 256),))
    short_lengths = place_ends(jax.random.randint(splits[12], (NSEG,), 1, SBLK + 1), jax.random.fold_in(splits[12], 1), 1, SBLK).astype(jnp.int32)
    gap_short = place_ends(jax.random.randint(splits[13], (SHORT,), 0, NBK), jax.random.fold_in(splits[13], 1), 0, NBK - 1).astype(jnp.int32)
    bias_table = noise(splits[14], (H, NBK), 1.0, 4.0, (), jnp.float32)
    return {"q_long": q_long, "k_long": k_long, "v_long": v_long, "out_long": out_long, "grad_long": grad_long, "cycle_group": cycle_group, "gap_long": gap_long, "q_short": q_short, "k_short": k_short, "v_short": v_short, "out_short": out_short, "grad_short": grad_short, "short_lengths": short_lengths, "gap_short": gap_short, "bias_table": bias_table}


NEG = -1.0e30


def attend_grads(query, keys, values, outv, grad3, allowed, row_live, key_bias):
    scale = HD ** -0.5
    qf = query.astype(jnp.float32)
    kf = keys.astype(jnp.float32)
    vf = values.astype(jnp.float32)
    of = outv.astype(jnp.float32)
    gf = grad3.astype(jnp.float32)
    scores = jnp.einsum('ihd,jhd->hij', qf, kf) * scale + key_bias[:, None, :]
    scores = jnp.where(allowed[None], scores, NEG)
    top = jnp.max(scores, axis=-1, keepdims=True)
    weights = jnp.where(allowed[None], jnp.exp(scores - top), 0.0)
    total = jnp.sum(weights, axis=-1, keepdims=True)
    probs = jnp.where(row_live[None, :, None], weights / total, 0.0)
    probs_low = lax.optimization_barrier(probs.astype(jnp.bfloat16)).astype(jnp.float32)
    dprobs = jnp.einsum('ihd,jhd->hij', gf, vf)
    delta = jnp.einsum('ihd,ihd->hi', gf, of)
    dscores = probs * (dprobs - delta[:, :, None])
    dlow = lax.optimization_barrier(dscores.astype(jnp.bfloat16)).astype(jnp.float32)
    dquery = jnp.einsum('hij,jhd->ihd', dlow, kf) * scale
    dkeys = jnp.einsum('hij,ihd->jhd', dlow, qf) * scale
    dvalues = jnp.einsum('hij,ihd->jhd', probs_low, gf)
    column = jnp.sum(dscores, axis=1)
    return dquery, dkeys, dvalues, column


def bucket_sum(column, gaps):
    return jax.ops.segment_sum(column.T, gaps, num_segments=NBK).T


def long_row(operands, bias_table):
    q_row, k_row, v_row, out_row, grad_row, groups, gaps = operands
    pad = WIN - 1
    key_bias = bias_table[:, gaps]
    zeros_kv = jnp.zeros((pad * S_DEV, D), jnp.bfloat16)
    k_pad = jnp.concatenate([zeros_kv, k_row], axis=0)
    v_pad = jnp.concatenate([zeros_kv, v_row], axis=0)
    group_pad = jnp.concatenate([jnp.full((pad,), -1, jnp.int32), groups.astype(jnp.int32)])
    gaps_pad = jnp.concatenate([jnp.zeros((pad * S_DEV,), jnp.int32), gaps.astype(jnp.int32)])
    bias_pad = jnp.concatenate([jnp.zeros((H, pad * S_DEV), jnp.float32), key_bias], axis=1)
    window = WIN * S_DEV
    slot = jnp.arange(window, dtype=jnp.int32) // S_DEV
    inner = jnp.arange(window, dtype=jnp.int32) % S_DEV
    rows = jnp.arange(S_DEV, dtype=jnp.int32)

    def shard(index):
        start = (index * S_DEV).astype(jnp.int32)
        query = lax.dynamic_slice_in_dim(q_row, start, S_DEV).reshape(S_DEV, H, HD)
        outv = lax.dynamic_slice_in_dim(out_row, start, S_DEV).reshape(S_DEV, H, HD)
        grad3 = lax.dynamic_slice_in_dim(grad_row, start, S_DEV).reshape(S_DEV, H, HD)
        keys = lax.dynamic_slice_in_dim(k_pad, start, window).reshape(window, H, HD)
        values = lax.dynamic_slice_in_dim(v_pad, start, window).reshape(window, H, HD)
        window_groups = lax.dynamic_slice_in_dim(group_pad, index.astype(jnp.int32), WIN)
        own = lax.dynamic_index_in_dim(groups.astype(jnp.int32), index.astype(jnp.int32), keepdims=False)
        same = (window_groups[slot] == own)[None, :]
        earlier = (slot < WIN - 1)[None, :]
        allowed = same & (earlier | (inner[None, :] <= rows[:, None]))
        bias_w = lax.dynamic_slice_in_dim(bias_pad, start, window, axis=1)
        gaps_w = lax.dynamic_slice_in_dim(gaps_pad, start, window)
        live = jnp.full((S_DEV,), True)
        dquery, dkeys, dvalues, column = attend_grads(query, keys, values, outv, grad3, allowed, live, bias_w)
        return dquery.reshape(S_DEV, D), dkeys.reshape(window, D), dvalues.reshape(window, D), bucket_sum(column, gaps_w)

    dq_all, dk_all, dv_all, dbias_all = lax.map(shard, jnp.arange(N_BLK, dtype=jnp.int32))
    dk_parts = dk_all.reshape(N_BLK, WIN, S_DEV, D)
    dv_parts = dv_all.reshape(N_BLK, WIN, S_DEV, D)
    dk_acc = jnp.zeros((N_BLK + pad, S_DEV, D), jnp.float32)
    dv_acc = jnp.zeros((N_BLK + pad, S_DEV, D), jnp.float32)
    for slot_index in range(WIN):
        dk_acc = dk_acc.at[slot_index:slot_index + N_BLK].add(dk_parts[:, slot_index])
        dv_acc = dv_acc.at[slot_index:slot_index + N_BLK].add(dv_parts[:, slot_index])
    grad_q = dq_all.reshape(L, D).astype(jnp.bfloat16)
    grad_k = dk_acc[pad:].reshape(L, D).astype(jnp.bfloat16)
    grad_v = dv_acc[pad:].reshape(L, D).astype(jnp.bfloat16)
    return grad_q, grad_k, grad_v, jnp.sum(dbias_all, axis=0)


def short_block(operands, bias_table):
    query, keys, values, outv, grad3, length, gaps = operands
    rows = jnp.arange(SBLK, dtype=jnp.int32)
    allowed = (rows[None, :] <= rows[:, None]) & (rows[None, :] < length)
    live = rows < length
    key_bias = bias_table[:, gaps]
    dquery, dkeys, dvalues, column = attend_grads(
        query.reshape(SBLK, H, HD), keys.reshape(SBLK, H, HD), values.reshape(SBLK, H, HD),
        outv.reshape(SBLK, H, HD), grad3.reshape(SBLK, H, HD), allowed, live, key_bias)
    return (dquery.reshape(SBLK, D).astype(jnp.bfloat16), dkeys.reshape(SBLK, D).astype(jnp.bfloat16),
            dvalues.reshape(SBLK, D).astype(jnp.bfloat16), bucket_sum(column, gaps))


def reference(q_long, k_long, v_long, out_long, grad_long, cycle_group, gap_long, q_short, k_short, v_short, out_short, grad_short, short_lengths, gap_short, bias_table):
    long_q, long_k, long_v, long_bias = lax.map(
        lambda ops: long_row(ops, bias_table),
        (q_long, k_long, v_long, out_long, grad_long, cycle_group, gap_long))

    def shaped(x):
        return x.reshape(NSEG, SBLK, D)

    short_q, short_k, short_v, short_bias = lax.map(
        lambda ops: short_block(ops, bias_table),
        (shaped(q_short), shaped(k_short), shaped(v_short), shaped(out_short), shaped(grad_short),
         short_lengths, gap_short.reshape(NSEG, SBLK)))
    grad_bias = jnp.sum(long_bias, axis=0) + jnp.sum(short_bias, axis=0)
    return (long_q, long_k, long_v, short_q.reshape(SHORT, D), short_k.reshape(SHORT, D),
            short_v.reshape(SHORT, D), grad_bias)
```

```python
import functools
import math

import jax
import jax.numpy as jnp
from jax import lax
from jax.experimental import pallas as pl
from jax.experimental.pallas import tpu as pltpu
from jax.sharding import PartitionSpec as P

NEG = -1e30
LOG2E = math.log2(math.e)
MESH = pl.DeviceIdType.MESH
RING = 4
WIN = 4
Q, G, K, V = 0, 1, 2, 3
F32 = jnp.float32
BF16 = jnp.bfloat16


def dot_nn(a, b):
    return lax.dot_general(a, b, (((1,), (0,)), ((), ())), preferred_element_type=F32)


def dot_nt(a, b):
    return lax.dot_general(a, b, (((1,), (1,)), ((), ())), preferred_element_type=F32)


def dot_tn(a, b):
    return lax.dot_general(a, b, (((0,), (0,)), ((), ())), preferred_element_type=F32)


def halves(value):
    high = value.astype(BF16)
    return high, (value - high.astype(F32)).astype(BF16)


def row_pick(row, count=8, width=128):
    rows = lax.broadcasted_iota(jnp.int32, (count, width), 0)
    return jnp.where(rows == row, 1.0, 0.0).astype(BF16)


def lane_sums(value, row):
    pick = row_pick(row)
    high, low = halves(value)
    return dot_nt(pick, high) + dot_nt(pick, low)


def bucket_sums(column, onehot):
    high, low = halves(column)
    return dot_nt(high, onehot) + dot_nt(low, onehot)


def kernel(
    dp_size,
    q_ref, k_ref, v_ref, o_ref, g_ref, group_ref, gap_ref,
    qs_ref, ks_ref, vs_ref, os_ref, gs_ref, len_ref, gaps_ref, table_ref,
    gq_ref, gk_ref, gv_ref, gqs_ref, gks_ref, gvs_ref, gb_ref,
    qb, gb, kb, vb, g_own, o_own, delta_buf, stat_out, stat_in,
    qs, ks, vs, os, gs, dqs, dks, dvs,
    dq_out, dk_out, dv_out, dk_sum, dv_sum, bias_sum,
    bias_rows, bias_cols, reduce_buf,
    load_sem, a2a_send, a2a_recv, delta_send, delta_recv, z_send, z_recv,
    stat_send, stat_recv, out_send, out_recv, own_sem, red_send, red_recv, store_sem,
):
    dp = lax.axis_index("dp")
    blk = lax.axis_index("blk")
    x = blk % RING
    z = blk // RING
    planes = 4
    span = 128
    depth = 128
    heads = table_ref.shape[0]
    mine = heads // RING
    wide = mine * depth
    scale = depth ** (-0.5)
    score_scale = scale * LOG2E
    halo = WIN - 1

    bufs = (qb, gb, kb, vb)
    ins = (q_ref, g_ref, k_ref, v_ref)
    base = (0, 0, halo, halo)

    def rows(n):
        if isinstance(n, int):
            return pl.ds(n * span, span)
        return pl.ds(pl.multiple_of(n * span, span), span)

    def at(zz, xx):
        return (dp, zz * RING + xx)

    up, down = (z + 1) % planes, (z + planes - 1) % planes

    peers = []
    for r in range(1, RING):
        peers.append(at(z, (x + r) % RING))
        peers.append(at((z + r) % planes, x))
    stages = [
        (x, lambda r: at(z, (x + r) % RING)),
        (z, lambda r: at((z + r) % planes, x)),
    ]
    if dp_size > 1:
        y, c4 = dp // 4, dp % 4
        stages.append((y, lambda r: (((y + r) % 4) * 4 + c4, blk)))
        stages.append((c4, lambda r: (y * 4 + (c4 + r) % 4, blk)))
        for r in range(1, 4):
            peers.append((((y + r) % 4) * 4 + c4, blk))
            peers.append((y * 4 + (c4 + r) % 4, blk))

    def own_cols(ref, xx):
        return ref.at[0, :, pl.ds(pl.multiple_of(xx * wide, wide), wide)]

    def a2a(t, r):
        to = (x + r) % RING
        return pltpu.make_async_remote_copy(
            src_ref=own_cols(ins[t], to),
            dst_ref=bufs[t].at[rows(base[t] + x)],
            send_sem=a2a_send.at[t, r - 1], recv_sem=a2a_recv.at[t, r - 1],
            device_id=at(z, to), device_id_type=MESH,
        )

    def own_load(t):
        return pltpu.make_async_copy(own_cols(ins[t], x), bufs[t].at[rows(base[t] + x)], load_sem.at[t])

    def across(t, c, own):
        src = own_cols(ins[t], x) if own else bufs[t].at[rows(base[t] + c)]
        if t in (Q, G):
            slot, index, to = RING + c, c, down
        else:
            slot, index, to = c - 1, c - 1, up
        return pltpu.make_async_remote_copy(
            src_ref=src, dst_ref=bufs[t].at[rows(slot)],
            send_sem=z_send.at[t, index], recv_sem=z_recv.at[t, index],
            device_id=at(to, x), device_id_type=MESH,
        )

    def crosses(t, c):
        return c <= halo - 1 if t in (Q, G) else c >= 1

    def delta_copy(r):
        return pltpu.make_async_remote_copy(
            src_ref=delta_buf.at[x], dst_ref=delta_buf.at[x],
            send_sem=delta_send.at[r - 1], recv_sem=delta_recv.at[r - 1],
            device_id=at(z, (x + r) % RING), device_id_type=MESH,
        )

    def stat_copy(c):
        return pltpu.make_async_remote_copy(
            src_ref=stat_out.at[c], dst_ref=stat_in.at[c],
            send_sem=stat_send.at[c], recv_sem=stat_recv.at[c],
            device_id=at(down, x), device_id_type=MESH,
        )

    stage_bufs = (dq_out, dk_out, dv_out)
    outs = (gq_ref, gk_ref, gv_ref)

    def out_copy(t, c):
        return pltpu.make_async_remote_copy(
            src_ref=stage_bufs[t].at[rows(c)], dst_ref=own_cols(outs[t], x),
            send_sem=out_send.at[t, c], recv_sem=out_recv.at[t, x],
            device_id=at(z, c), device_id_type=MESH,
        )

    def out_arrival(t, r):
        source = (x + r) % RING
        return pltpu.make_async_remote_copy(
            src_ref=stage_bufs[t].at[rows(0)], dst_ref=own_cols(outs[t], source),
            send_sem=out_send.at[t, 0], recv_sem=out_recv.at[t, source],
            device_id=at(z, source), device_id_type=MESH,
        )

    def out_own(t, c):
        return pltpu.make_async_copy(stage_bufs[t].at[rows(c)], own_cols(outs[t], x), own_sem.at[t])

    def send_out(t, c):
        @pl.when(x == c)
        def _():
            out_own(t, c).start()

        @pl.when(x != c)
        def _():
            out_copy(t, c).start()

    loads = [own_load(t) for t in range(4)]
    loads.append(pltpu.make_async_copy(g_ref.at[0], g_own, load_sem.at[4]))
    loads.append(pltpu.make_async_copy(o_ref.at[0], o_own, load_sem.at[5]))
    short_loads = [
        pltpu.make_async_copy(src, dst, load_sem.at[6 + n])
        for n, (src, dst) in enumerate(
            ((qs_ref, qs), (ks_ref, ks), (vs_ref, vs), (os_ref, os), (gs_ref, gs))
        )
    ]
    for copy in loads[4:] + short_loads + loads[:4]:
        copy.start()

    barrier = pltpu.get_barrier_semaphore()
    for peer in peers:
        pl.semaphore_signal(barrier, inc=1, device_id=peer, device_id_type=MESH)
    pl.semaphore_wait(barrier, len(peers))

    order = (1, 3, 2)
    for t in range(4):
        for r in order:
            a2a(t, r).start()

        @pl.when(crosses(t, x))
        def _(t=t):
            across(t, x, True).start()

    loads[4].wait()
    loads[5].wait()
    delta = jnp.zeros((8, span), F32)
    for h in range(heads):
        cols = pl.ds(h * depth, depth)
        delta = delta + lane_sums(g_own[:, cols].astype(F32) * o_own[:, cols].astype(F32), h)
    delta_buf[x] = delta
    for r in order:
        delta_copy(r).start()

    table = table_ref[...] * LOG2E
    buckets = lax.broadcasted_iota(jnp.int32, (table.shape[1], span), 0)
    buckets_wide = lax.broadcasted_iota(jnp.int32, (128, span), 0)

    def bias_of(gaps):
        onehot = jnp.where(buckets == gaps, 1.0, 0.0)
        return jnp.dot(table, onehot, precision=lax.Precision.HIGHEST, preferred_element_type=F32)

    def long_gaps(n):
        shard = (z * RING + n - halo + 16) % 16
        return gap_ref[:, rows(shard)]

    bias_cols[...] = jnp.zeros((128, 128), F32)
    for n in range(halo + RING):
        bias_rows[...] = bias_of(long_gaps(n))
        for h in range(mine):
            bias_cols[pl.ds(n * mine + h, 1), :] = bias_rows[pl.ds(x * mine + h, 1), :]
    for b in range(2):
        bias_cols[pl.ds(16 + 8 * b, 8), :] = bias_of(gaps_ref[:, rows(b)])
    bias_cols[...] = bias_cols[...].T

    key_rows = lax.broadcasted_iota(jnp.int32, (span, span), 0)
    query_cols = lax.broadcasted_iota(jnp.int32, (span, span), 1)
    causal = key_rows <= query_cols

    for copy in short_loads:
        copy.wait()

    def short_step(step, columns):
        columns = list(columns)
        for b in range(2):
            length = len_ref[b]
            allowed = causal & (key_rows < length)
            live = lax.broadcasted_iota(jnp.int32, (1, span), 1) < length
            for inner in range(2):
                h = step * 2 + inner
                cols = pl.ds(h * depth, depth)
                r = rows(b)
                bias = jnp.sum(
                    jnp.where(query_cols == 16 + 8 * b + h, bias_cols[...], 0.0), axis=1, keepdims=True
                )
                query, keys, values, grad = qs[r, cols], ks[r, cols], vs[r, cols], gs[r, cols]
                prod = grad.astype(F32) * os[r, cols].astype(F32)
                delta = lane_sums(prod, 0)[0:1]
                scores = dot_nt(keys, query) * score_scale + bias
                scores = jnp.where(allowed, scores, NEG)
                top = jnp.max(scores, axis=0, keepdims=True)
                weights = jnp.exp2(scores - top)
                inverse = 1.0 / jnp.sum(weights, axis=0, keepdims=True)
                probs = weights * jnp.where(live, inverse, 0.0)
                dprobs = dot_nt(values, grad)
                dscores = probs * (dprobs - delta)
                dlow = dscores.astype(BF16)
                dqs[r, cols] = (dot_tn(dlow, keys) * scale).astype(BF16)
                dks[r, cols] = (dot_nn(dlow, query) * scale).astype(BF16)
                dvs[r, cols] = dot_nn(probs.astype(BF16), grad).astype(BF16)
                columns[b] = columns[b] + lane_sums(dscores, h)
        return tuple(columns)

    zero_col = jnp.zeros((8, span), F32)
    short_columns = (zero_col, zero_col)

    def forward(t, r):
        a2a(t, r).wait_recv()
        c = (x + RING - r) % RING

        @pl.when(crosses(t, c))
        def _():
            across(t, c, False).start()

    for step in range(4):
        short_columns = short_step(step, short_columns)
        for r in order:
            forward(step, r)

    stores = [
        pltpu.make_async_copy(src, dst, store_sem.at[n])
        for n, (src, dst) in enumerate(((dqs, gqs_ref), (dks, gks_ref), (dvs, gvs_ref)))
    ]
    for copy in stores:
        copy.start()

    local_bias = jnp.zeros((8, 128), F32)
    for b in range(2):
        onehot = jnp.where(buckets_wide == gaps_ref[:, rows(b)], 1.0, 0.0).astype(BF16)
        local_bias = local_bias + bucket_sums(short_columns[b], onehot)

    for copy in loads[:4]:
        copy.wait()
    for r in order:
        delta_copy(r).wait_recv()

    def penalty(query_shard, key_shard):
        there = (query_shard < 16) & (key_shard >= 0)
        same = group_ref[0, (query_shard + 16) % 16] == group_ref[0, (key_shard + 16) % 16]
        return jnp.where(there & same, 0.0, NEG).astype(F32)

    def bias_col(n, h):
        return bias_cols[:, pl.ds(n * mine + h, 1)]

    started = set()

    def add_to(ref, k, h, value):
        cols = pl.ds(h * depth, depth)
        if (id(ref), k, h) in started:
            ref[rows(k), cols] += value
        else:
            started.add((id(ref), k, h))
            ref[rows(k), cols] = value

    def query_home(c):
        for h in range(mine):
            cols = pl.ds(h * depth, depth)
            query, grad = qb[rows(c), cols], gb[rows(c), cols]
            delta = delta_buf[c, pl.ds(x * mine + h, 1), :]
            scores = []
            for w in range(WIN):
                n = c + w
                pen = penalty(z * RING + c, z * RING + n - halo)
                s = dot_nt(kb[rows(n), cols], query) * score_scale + (bias_col(n, h) + pen)
                if w == WIN - 1:
                    s = jnp.where(causal, s, NEG)
                scores.append(s)
            top = scores[0]
            for s in scores[1:]:
                top = jnp.maximum(top, s)
            top = jnp.max(top, axis=0, keepdims=True)
            weights = [jnp.exp2(s - top) for s in scores]
            total = weights[0]
            for weight in weights[1:]:
                total = total + weight
            inverse = 1.0 / jnp.sum(total, axis=0, keepdims=True)
            if c < halo:
                stat_out[c, pl.ds(h, 1), :] = top
                stat_out[c, pl.ds(2 + h, 1), :] = inverse
                stat_out[c, pl.ds(4 + h, 1), :] = delta
            dquery = jnp.zeros((span, depth), F32)
            for w in range(WIN):
                n = c + w
                probs = weights[w] * inverse
                dscores = probs * (dot_nt(vb[rows(n), cols], grad) - delta)
                dlow = dscores.astype(BF16)
                dquery = dquery + dot_tn(dlow, kb[rows(n), cols])
                if n >= halo:
                    k = n - halo
                    add_to(dv_sum, k, h, dot_nn(probs.astype(BF16), grad))
                    add_to(dk_sum, k, h, dot_nn(dlow, query))
                    add_to(bias_sum, k, h, dscores)
            dq_out[rows(c), cols] = (dquery * scale).astype(BF16)
        if c < halo:
            stat_copy(c).start()
        send_out(0, c)

    def key_home(c):
        for h in range(mine):
            cols = pl.ds(h * depth, depth)
            query, grad = qb[rows(RING + c), cols], gb[rows(RING + c), cols]
            top = stat_in[c, pl.ds(h, 1), :]
            inverse = stat_in[c, pl.ds(2 + h, 1), :]
            delta = stat_in[c, pl.ds(4 + h, 1), :]
            for k in range(c + 1, RING):
                n = k + halo
                pen = penalty((z + 1) * RING + c, z * RING + k)
                s = dot_nt(kb[rows(n), cols], query) * score_scale + (bias_col(n, h) + pen)
                probs = jnp.exp2(s - top) * inverse
                dscores = probs * (dot_nt(vb[rows(n), cols], grad) - delta)
                add_to(dv_sum, k, h, dot_nn(probs.astype(BF16), grad))
                add_to(dk_sum, k, h, dot_nn(dscores.astype(BF16), query))
                add_to(bias_sum, k, h, dscores)

    def finish(k):
        dk_out[rows(k), :] = (dk_sum[rows(k), :] * scale).astype(BF16)
        dv_out[rows(k), :] = dv_sum[rows(k), :].astype(BF16)
        send_out(1, k)
        send_out(2, k)

    query_home(3)
    for c in (2, 1, 0):
        for t in (K, V):
            across(t, c + 1, False).wait_recv()
        query_home(c)
    finish(0)
    for c in range(halo):
        for t in (Q, G):
            across(t, c, False).wait_recv()
        stat_copy(c).wait_recv()
        key_home(c)
        finish(c + 1)

    for k in range(RING):
        onehot = jnp.where(buckets_wide == long_gaps(k + halo), 1.0, 0.0).astype(BF16)
        column = zero_col
        for h in range(mine):
            column = column + lane_sums(bias_sum[rows(k), pl.ds(h * depth, depth)], x * mine + h)
        local_bias = local_bias + bucket_sums(column, onehot)

    value = local_bias
    for s, (place, peer) in enumerate(stages):
        reduce_buf[s, place] = value
        copies = [
            pltpu.make_async_remote_copy(
                src_ref=reduce_buf.at[s, place], dst_ref=reduce_buf.at[s, place],
                send_sem=red_send.at[s, r - 1], recv_sem=red_recv.at[s, r - 1],
                device_id=peer(r), device_id_type=MESH,
            )
            for r in range(1, 4)
        ]
        for copy in copies:
            copy.start()
        for copy in copies:
            copy.wait_recv()
        value = (reduce_buf[s, 0] + reduce_buf[s, 1]) + (reduce_buf[s, 2] + reduce_buf[s, 3])
        for copy in copies:
            copy.wait_send()
    gb_ref[...] = value[:, : gb_ref.shape[1]]

    for t in range(3):
        out_own(t, 0).wait()
        for c in range(RING):

            @pl.when(x != c)
            def _(t=t, c=c):
                out_copy(t, c).wait_send()

        for r in range(1, RING):
            out_arrival(t, r).wait_recv()
    for c in range(halo):
        stat_copy(c).wait_send()
    for r in order:
        delta_copy(r).wait_send()
    for t in range(4):
        for r in order:
            a2a(t, r).wait_send()
        for index in range(halo):
            across(t, index if t in (Q, G) else index + 1, False).wait_send()
    for copy in stores:
        copy.wait()


def body(dp_size, q, k, v, o, g, groups, gap_long, qs, ks, vs, os, gs, lengths, gap_short, table):
    hbm = pl.BlockSpec(memory_space=pltpu.HBM)
    vmem = pl.BlockSpec(memory_space=pltpu.VMEM)
    smem = pl.BlockSpec(memory_space=pltpu.SMEM)
    span, width = q.shape[1:]
    rows = qs.shape[0]
    wide = width // RING
    dma = pltpu.SemaphoreType.DMA
    long_out = jax.ShapeDtypeStruct(q.shape, q.dtype)
    short_out = jax.ShapeDtypeStruct(qs.shape, qs.dtype)
    return pl.pallas_call(
        functools.partial(kernel, dp_size),
        out_shape=(long_out,) * 3 + (short_out,) * 3 + (jax.ShapeDtypeStruct(table.shape, F32),),
        in_specs=[hbm] * 5 + [smem, vmem] + [hbm] * 5 + [smem, vmem, vmem],
        out_specs=(hbm,) * 6 + (vmem,),
        scratch_shapes=[pltpu.VMEM((7 * span, wide), BF16)] * 4
        + [pltpu.VMEM((span, width), BF16)] * 2
        + [pltpu.VMEM((4, 8, 128), F32), pltpu.VMEM((3, 8, 128), F32), pltpu.VMEM((3, 8, 128), F32)]
        + [pltpu.VMEM((rows, width), BF16)] * 8
        + [pltpu.VMEM((4 * span, wide), BF16)] * 3
        + [pltpu.VMEM((4 * span, wide), F32)] * 3
        + [pltpu.VMEM((8, 128), F32), pltpu.VMEM((128, 128), F32), pltpu.VMEM((4, 4, 8, 128), F32)]
        + [
            dma((11,)), dma((4, 3)), dma((4, 3)), dma((3,)), dma((3,)), dma((4, 3)), dma((4, 3)),
            dma((3,)), dma((3,)), dma((3, 4)), dma((3, 4)), dma((3,)), dma((4, 3)), dma((4, 3)), dma((3,)),
        ],
        compiler_params=pltpu.CompilerParams(
            collective_id=0, has_side_effects=True, vmem_limit_bytes=56 * 1024 * 1024
        ),
        name="window_grads",
    )(q, k, v, o, g, groups, gap_long, qs, ks, vs, os, gs, lengths, gap_short.reshape(1, -1), table)


def solution(mesh):
    placed = (
        (P("dp", "blk", None),) * 5
        + (P("dp", None), P("dp", None))
        + (P(("dp", "blk"), None),) * 5
        + (P(("dp", "blk")), P(("dp", "blk")), P())
    )
    return jax.shard_map(
        functools.partial(body, mesh.shape["dp"]),
        mesh=mesh,
        in_specs=placed,
        out_specs=(P("dp", "blk", None),) * 3 + (P(("dp", "blk"), None),) * 3 + (P(),),
        check_vma=False,
    )
```

```python
import functools
import math

import jax
import jax.numpy as jnp
from jax import lax
from jax.experimental import pallas as pl
from jax.experimental.pallas import tpu as pltpu
from jax.sharding import PartitionSpec as P

NEG = -1e30
LOG2E = math.log2(math.e)
MESH = pl.DeviceIdType.MESH
RING = 4
WIN = 4
Q, G, K, V = 0, 1, 2, 3
F32 = jnp.float32
VMEM_LIMIT = 56 * 1024 * 1024
BF16 = jnp.bfloat16


def dot_nn(a, b):
    return lax.dot_general(a, b, (((1,), (0,)), ((), ())), preferred_element_type=F32)


def dot_nt(a, b):
    return lax.dot_general(a, b, (((1,), (1,)), ((), ())), preferred_element_type=F32)


def dot_tn(a, b):
    return lax.dot_general(a, b, (((0,), (0,)), ((), ())), preferred_element_type=F32)


def halves(value):
    high = value.astype(BF16)
    return high, (value - high.astype(F32)).astype(BF16)


def row_pick(row, count=8, width=128):
    rows = lax.broadcasted_iota(jnp.int32, (count, width), 0)
    return jnp.where(rows == row, 1.0, 0.0).astype(BF16)


def lane_sums(value, row):
    pick = row_pick(row)
    high, low = halves(value)
    return dot_nt(pick, high) + dot_nt(pick, low)


def bucket_sums(column, onehot):
    high, low = halves(column)
    return dot_nt(high, onehot) + dot_nt(low, onehot)


def place_kernel(*refs):
    count = (len(refs) - 2) // 3
    ins, outs, held = refs[:count], refs[count : 2 * count], refs[2 * count : 3 * count]
    in_sem, out_sem = refs[3 * count :]
    loads = [pltpu.make_async_copy(ins[n], held[n], in_sem.at[n]) for n in range(count)]
    stores = [pltpu.make_async_copy(held[n], outs[n], out_sem.at[n]) for n in range(count)]
    for copy in loads:
        copy.start()
    for load, store in zip(loads, stores):
        load.wait()
        store.start()
    for copy in stores:
        copy.wait()


def kernel(
    dp_size,
    q_ref, k_ref, v_ref, o_ref, g_ref, group_ref, gap_ref,
    qs_ref, ks_ref, vs_ref, os_ref, gs_ref, len_ref, gaps_ref, table_ref,
    gq_ref, gk_ref, gv_ref, gqs_ref, gks_ref, gvs_ref, gb_ref,
    qb, gb, kb, vb, g_own, o_own, delta_buf, stat_out, stat_in,
    qs, ks, vs, os, gs, dqs, dks, dvs,
    dq_out, dk_out, dv_out, dq_sum, dk_sum, dv_sum, bias_sum, probs_buf,
    bias_rows, bias_cols, reduce_buf,
    load_sem, a2a_send, a2a_recv, delta_send, delta_recv, z_send, z_recv,
    stat_send, stat_recv, out_send, out_recv, own_sem, red_send, red_recv, store_sem,
):
    dp = lax.axis_index("dp")
    blk = lax.axis_index("blk")
    x = blk % RING
    z = blk // RING
    planes = 4
    span = 128
    depth = 128
    heads = table_ref.shape[0]
    mine = heads // RING
    wide = mine * depth
    scale = depth ** (-0.5)
    score_scale = scale * LOG2E
    halo = WIN - 1

    bufs = (qb, gb, kb, vb)
    ins = (q_ref, g_ref, k_ref, v_ref)
    base = (0, 0, halo, halo)

    def rows(n):
        if isinstance(n, int):
            return pl.ds(n * span, span)
        return pl.ds(pl.multiple_of(n * span, span), span)

    def at(zz, xx):
        return (dp, zz * RING + xx)

    up, down = (z + 1) % planes, (z + planes - 1) % planes

    y, c4 = (dp // 4, dp % 4) if dp_size > 1 else (0, 0)
    y_size, c_size = (4, 4) if dp_size > 1 else (1, 1)

    def across_plane(dy, dx):
        yy, xx = (y + dy) % y_size, (x + dx) % RING
        return (yy * 4 + c4, z * RING + xx), yy * RING + xx

    def across_planes(dz, dc):
        zz, cc = (z + dz) % planes, (c4 + dc) % c_size
        return (y * 4 + cc, zz * RING + x), zz * c_size + cc

    stages = [
        (y * RING + x, y_size * RING, [across_plane(a, b)[0] for a in range(y_size) for b in range(RING) if a or b]),
        (z * c_size + c4, planes * c_size, [across_planes(a, b)[0] for a in range(planes) for b in range(c_size) if a or b]),
    ]
    peers = stages[0][2] + stages[1][2]

    def own_cols(ref, xx):
        return ref.at[0, :, pl.ds(pl.multiple_of(xx * wide, wide), wide)]

    def a2a(t, to):
        return pltpu.make_async_remote_copy(
            src_ref=own_cols(ins[t], to),
            dst_ref=bufs[t].at[rows(base[t] + x)],
            send_sem=a2a_send.at[t, to], recv_sem=a2a_recv.at[t, x],
            device_id=at(z, to), device_id_type=MESH,
        )

    def a2a_arrival(t, source):
        return pltpu.make_async_remote_copy(
            src_ref=own_cols(ins[t], source),
            dst_ref=bufs[t].at[rows(base[t] + source)],
            send_sem=a2a_send.at[t, source], recv_sem=a2a_recv.at[t, source],
            device_id=at(z, source), device_id_type=MESH,
        )

    def own_load(t):
        return pltpu.make_async_copy(own_cols(ins[t], x), bufs[t].at[rows(base[t] + x)], load_sem.at[t])

    def across(t, c, own):
        src = own_cols(ins[t], x) if own else bufs[t].at[rows(base[t] + c)]
        if t in (Q, G):
            slot, index, to = RING + c, c, down
        else:
            slot, index, to = c - 1, c - 1, up
        return pltpu.make_async_remote_copy(
            src_ref=src, dst_ref=bufs[t].at[rows(slot)],
            send_sem=z_send.at[t, index], recv_sem=z_recv.at[t, index],
            device_id=at(to, x), device_id_type=MESH,
        )

    def crosses(t, c):
        return c <= halo - 1 if t in (Q, G) else c >= 1

    def delta_copy(r):
        return pltpu.make_async_remote_copy(
            src_ref=delta_buf.at[x], dst_ref=delta_buf.at[x],
            send_sem=delta_send.at[r - 1], recv_sem=delta_recv.at[r - 1],
            device_id=at(z, (x + r) % RING), device_id_type=MESH,
        )

    def stat_copy(c):
        return pltpu.make_async_remote_copy(
            src_ref=stat_out.at[c], dst_ref=stat_in.at[c],
            send_sem=stat_send.at[c], recv_sem=stat_recv.at[c],
            device_id=at(down, x), device_id_type=MESH,
        )

    stage_bufs = (dq_out, dk_out, dv_out)
    outs = (gq_ref, gk_ref, gv_ref)

    def out_copy(t, c):
        return pltpu.make_async_remote_copy(
            src_ref=stage_bufs[t].at[rows(c)], dst_ref=own_cols(outs[t], x),
            send_sem=out_send.at[t, c], recv_sem=out_recv.at[t, x],
            device_id=at(z, c), device_id_type=MESH,
        )

    def out_arrival(t, r):
        source = (x + r) % RING
        return pltpu.make_async_remote_copy(
            src_ref=stage_bufs[t].at[rows(0)], dst_ref=own_cols(outs[t], source),
            send_sem=out_send.at[t, 0], recv_sem=out_recv.at[t, source],
            device_id=at(z, source), device_id_type=MESH,
        )

    def out_own(t, c):
        return pltpu.make_async_copy(stage_bufs[t].at[rows(c)], own_cols(outs[t], x), own_sem.at[t])

    def send_out(t, c):
        @pl.when(x == c)
        def _():
            out_own(t, c).start()

        @pl.when(x != c)
        def _():
            out_copy(t, c).start()

    loads = [own_load(t) for t in range(4)]
    loads.append(pltpu.make_async_copy(g_ref.at[0], g_own, load_sem.at[4]))
    loads.append(pltpu.make_async_copy(o_ref.at[0], o_own, load_sem.at[5]))
    short_loads = [
        pltpu.make_async_copy(src, dst, load_sem.at[6 + n])
        for n, (src, dst) in enumerate(
            ((qs_ref, qs), (ks_ref, ks), (vs_ref, vs), (os_ref, os), (gs_ref, gs))
        )
    ]
    for copy in loads[4:] + short_loads + loads[:4]:
        copy.start()

    barrier = pltpu.get_barrier_semaphore()
    for peer in peers:
        pl.semaphore_signal(barrier, inc=1, device_id=peer, device_id_type=MESH)
    pl.semaphore_wait(barrier, len(peers))

    order = (1, 3, 2)
    for t in (K, Q, V, G):

        @pl.when(crosses(t, x))
        def _(t=t):
            across(t, x, True).start()

    for first, second in ((K, Q), (V, G)):
        for n in range(RING):
            for t, to in ((first, n), (second, RING - 1 - n)):

                @pl.when(x != to)
                def _(t=t, to=to):
                    a2a(t, to).start()

    loads[4].wait()
    loads[5].wait()
    delta = jnp.zeros((8, span), F32)
    for h in range(heads):
        cols = pl.ds(h * depth, depth)
        delta = delta + lane_sums(g_own[:, cols].astype(F32) * o_own[:, cols].astype(F32), h)
    delta_buf[x] = delta
    for r in order:
        delta_copy(r).start()

    table = table_ref[...] * LOG2E
    buckets = lax.broadcasted_iota(jnp.int32, (table.shape[1], span), 0)
    buckets_wide = lax.broadcasted_iota(jnp.int32, (128, span), 0)

    def bias_of(gaps):
        onehot = jnp.where(buckets == gaps, 1.0, 0.0)
        return jnp.dot(table, onehot, precision=lax.Precision.HIGHEST, preferred_element_type=F32)

    def long_gaps(n):
        shard = (z * RING + n - halo + 16) % 16
        return gap_ref[:, rows(shard)]

    bias_cols[...] = jnp.zeros((128, 128), F32)
    for n in range(halo + RING):
        bias_rows[...] = bias_of(long_gaps(n))
        for h in range(mine):
            bias_cols[pl.ds(n * mine + h, 1), :] = bias_rows[pl.ds(x * mine + h, 1), :]
    for b in range(2):
        bias_cols[pl.ds(16 + 8 * b, 8), :] = bias_of(gaps_ref[:, rows(b)])
    bias_cols[...] = bias_cols[...].T

    key_rows = lax.broadcasted_iota(jnp.int32, (span, span), 0)
    query_cols = lax.broadcasted_iota(jnp.int32, (span, span), 1)
    causal = key_rows <= query_cols

    for copy in short_loads:
        copy.wait()

    def short_step(step, columns):
        columns = list(columns)
        for b in range(2):
            length = len_ref[b]
            allowed = causal & (key_rows < length)
            live = lax.broadcasted_iota(jnp.int32, (1, span), 1) < length
            for inner in range(2):
                h = step * 2 + inner
                cols = pl.ds(h * depth, depth)
                r = rows(b)
                bias = jnp.sum(
                    jnp.where(query_cols == 16 + 8 * b + h, bias_cols[...], 0.0), axis=1, keepdims=True
                )
                query, keys, values, grad = qs[r, cols], ks[r, cols], vs[r, cols], gs[r, cols]
                prod = grad.astype(F32) * os[r, cols].astype(F32)
                delta = lane_sums(prod, 0)[0:1]
                scores = dot_nt(keys, query) * score_scale + bias
                scores = jnp.where(allowed, scores, NEG)
                top = jnp.max(scores, axis=0, keepdims=True)
                weights = jnp.exp2(scores - top)
                inverse = 1.0 / jnp.sum(weights, axis=0, keepdims=True)
                probs = weights * jnp.where(live, inverse, 0.0)
                dprobs = dot_nt(values, grad)
                dscores = probs * (dprobs - delta)
                dlow = dscores.astype(BF16)
                dqs[r, cols] = (dot_tn(dlow, keys) * scale).astype(BF16)
                dks[r, cols] = (dot_nn(dlow, query) * scale).astype(BF16)
                dvs[r, cols] = dot_nn(probs.astype(BF16), grad).astype(BF16)
                columns[b] = columns[b] + lane_sums(dscores, h)
        return tuple(columns)

    zero_col = jnp.zeros((8, span), F32)
    short_columns = (zero_col, zero_col)

    def forward(t, c):
        @pl.when(x != c)
        def _():
            a2a_arrival(t, c).wait_recv()
            across(t, c, False).start()

    def forward_step(up_tensor, down_tensor, n):
        forward(up_tensor, RING - 1 - n)
        forward(down_tensor, n)

    def forward_rest(up_tensor, down_tensor):
        for t, c in ((up_tensor, 0), (down_tensor, RING - 1)):

            @pl.when(x != c)
            def _(t=t, c=c):
                a2a_arrival(t, c).wait_recv()

    short_columns = short_step(0, short_columns)
    forward_step(K, Q, 0)
    short_columns = short_step(1, short_columns)
    forward_step(K, Q, 1)
    forward_step(K, Q, 2)
    short_columns = short_step(2, short_columns)
    forward_step(V, G, 0)
    short_columns = short_step(3, short_columns)
    forward_step(V, G, 1)
    forward_step(V, G, 2)
    forward_rest(K, Q)
    forward_rest(V, G)

    stores = [
        pltpu.make_async_copy(src, dst, store_sem.at[n])
        for n, (src, dst) in enumerate(((dqs, gqs_ref), (dks, gks_ref), (dvs, gvs_ref)))
    ]
    for copy in stores:
        copy.start()

    local_bias = jnp.zeros((8, 128), F32)
    for b in range(2):
        onehot = jnp.where(buckets_wide == gaps_ref[:, rows(b)], 1.0, 0.0).astype(BF16)
        local_bias = local_bias + bucket_sums(short_columns[b], onehot)

    for copy in loads[:4]:
        copy.wait()
    for r in order:
        delta_copy(r).wait_recv()

    def penalty(query_shard, key_shard):
        there = (query_shard < 16) & (key_shard >= 0)
        same = group_ref[0, (query_shard + 16) % 16] == group_ref[0, (key_shard + 16) % 16]
        return jnp.where(there & same, 0.0, NEG).astype(F32)

    def bias_col(n, h):
        return bias_cols[:, pl.ds(n * mine + h, 1)]

    started = set()

    def add_to(ref, k, h, value):
        cols = pl.ds(h * depth, depth)
        if (id(ref), k, h) in started:
            ref[rows(k), cols] += value
        else:
            started.add((id(ref), k, h))
            ref[rows(k), cols] = value

    def probs_at(c, h, w):
        return pl.ds(((c * mine + h) * WIN + w) * span, span)

    def stats(c):
        for h in range(mine):
            cols = pl.ds(h * depth, depth)
            query = qb[rows(c), cols]
            scores = []
            for w in range(WIN):
                n = c + w
                pen = penalty(z * RING + c, z * RING + n - halo)
                s = dot_nt(kb[rows(n), cols], query) * score_scale + (bias_col(n, h) + pen)
                if w == WIN - 1:
                    s = jnp.where(causal, s, NEG)
                scores.append(s)
            top = scores[0]
            for s in scores[1:]:
                top = jnp.maximum(top, s)
            top = jnp.max(top, axis=0, keepdims=True)
            weights = [jnp.exp2(s - top) for s in scores]
            total = weights[0]
            for weight in weights[1:]:
                total = total + weight
            inverse = 1.0 / jnp.sum(total, axis=0, keepdims=True)
            for w in range(WIN):
                probs_buf[probs_at(c, h, w), :] = weights[w] * inverse
            if c < halo:
                stat_out[c, pl.ds(h, 1), :] = top
                stat_out[c, pl.ds(2 + h, 1), :] = inverse
                stat_out[c, pl.ds(4 + h, 1), :] = delta_buf[c, pl.ds(x * mine + h, 1), :]
        if c < halo:
            stat_copy(c).start()

    def pair(c, n, h):
        cols = pl.ds(h * depth, depth)
        grad = gb[rows(c), cols]
        delta = delta_buf[c, pl.ds(x * mine + h, 1), :]
        probs = probs_buf[probs_at(c, h, n - c), :]
        dscores = probs * (dot_nt(vb[rows(n), cols], grad) - delta)
        dlow = dscores.astype(BF16)
        add_to(dq_sum, c, h, dot_tn(dlow, kb[rows(n), cols]))
        if n > 0:
            add_to(bias_sum, n, h, dscores)
        if n >= halo:
            add_to(dv_sum, n - halo, h, dot_nn(probs.astype(BF16), grad))
            add_to(dk_sum, n - halo, h, dot_nn(dlow, qb[rows(c), cols]))

    def finish_query(c):
        dq_out[rows(c), :] = (dq_sum[rows(c), :] * scale).astype(BF16)
        send_out(0, c)

    def key_home(c):
        for h in range(mine):
            cols = pl.ds(h * depth, depth)
            query, grad = qb[rows(RING + c), cols], gb[rows(RING + c), cols]
            top = stat_in[c, pl.ds(h, 1), :]
            inverse = stat_in[c, pl.ds(2 + h, 1), :]
            delta = stat_in[c, pl.ds(4 + h, 1), :]
            for k in range(c + 1, RING):
                n = k + halo
                pen = penalty((z + 1) * RING + c, z * RING + k)
                s = dot_nt(kb[rows(n), cols], query) * score_scale + (bias_col(n, h) + pen)
                probs = jnp.exp2(s - top) * inverse
                dscores = probs * (dot_nt(vb[rows(n), cols], grad) - delta)
                add_to(dv_sum, k, h, dot_nn(probs.astype(BF16), grad))
                add_to(dk_sum, k, h, dot_nn(dscores.astype(BF16), query))
                if c == 0 and k == 1:
                    add_to(bias_sum, n, h, dscores)

    def finish(k):
        dk_out[rows(k), :] = (dk_sum[rows(k), :] * scale).astype(BF16)
        dv_out[rows(k), :] = dv_sum[rows(k), :].astype(BF16)
        send_out(1, k)
        send_out(2, k)

    def arrive(t, c):
        across(t, c, False).wait_recv()

    def query_cross(n):
        arrive(V, n + 1)
        for c in range(n + 1):
            for h in range(mine):
                pair(c, n, h)
        finish_query(n)

    def key_cross(c):
        arrive(Q, c)
        arrive(G, c)
        stat_copy(c).wait_recv()
        key_home(c)
        finish(c + 1)

    def reduce_copies(s):
        place, size, others = stages[s]
        return [
            pltpu.make_async_remote_copy(
                src_ref=reduce_buf.at[s, place], dst_ref=reduce_buf.at[s, place],
                send_sem=red_send.at[s, n], recv_sem=red_recv.at[s, n],
                device_id=other, device_id_type=MESH,
            )
            for n, other in enumerate(others)
        ]

    def reduce_start(s, value):
        reduce_buf[s, stages[s][0]] = value
        for copy in reduce_copies(s):
            copy.start()

    def reduce_end(s):
        for copy in reduce_copies(s):
            copy.wait_recv()
        value = reduce_buf[s, 0]
        for n in range(1, stages[s][1]):
            value = value + reduce_buf[s, n]
        return value

    stats(3)
    for c in (2, 1, 0):
        arrive(K, c + 1)
        stats(c)
    for c in (3, 0, 1, 2):
        for n in range(halo, c + halo + 1):
            for h in range(mine):
                pair(c, n, h)
        if c == 3:
            finish_query(3)
    finish(0)
    query_cross(2)
    key_cross(0)
    query_cross(1)

    for n in range(1, halo + RING):
        onehot = jnp.where(buckets_wide == long_gaps(n), 1.0, 0.0).astype(BF16)
        column = zero_col
        for h in range(mine):
            column = column + lane_sums(bias_sum[rows(n), pl.ds(h * depth, depth)], x * mine + h)
        local_bias = local_bias + bucket_sums(column, onehot)
    reduce_start(0, local_bias)

    key_cross(1)
    query_cross(0)
    key_cross(2)
    reduce_start(1, reduce_end(0))
    gb_ref[...] = reduce_end(1)[:, : gb_ref.shape[1]]

    for t in range(3):
        out_own(t, 0).wait()
        for c in range(RING):

            @pl.when(x != c)
            def _(t=t, c=c):
                out_copy(t, c).wait_send()

        for r in range(1, RING):
            out_arrival(t, r).wait_recv()
    for c in range(halo):
        stat_copy(c).wait_send()
    for r in order:
        delta_copy(r).wait_send()
    for s in range(2):
        for copy in reduce_copies(s):
            copy.wait_send()
    for t in range(4):
        for to in range(RING):

            @pl.when(x != to)
            def _(t=t, to=to):
                a2a(t, to).wait_send()

        for index in range(halo):
            across(t, index if t in (Q, G) else index + 1, False).wait_send()
    for copy in stores:
        copy.wait()


def body(dp_size, q, k, v, o, g, groups, gap_long, qs, ks, vs, os, gs, lengths, gap_short, table):
    hbm = pl.BlockSpec(memory_space=pltpu.HBM)
    vmem = pl.BlockSpec(memory_space=pltpu.VMEM)
    smem = pl.BlockSpec(memory_space=pltpu.SMEM)
    span, width = q.shape[1:]
    rows = qs.shape[0]
    wide = width // RING
    dma = pltpu.SemaphoreType.DMA
    long_out = jax.ShapeDtypeStruct(q.shape, q.dtype)
    short_out = jax.ShapeDtypeStruct(qs.shape, qs.dtype)
    shapes = (long_out,) * 3 + (short_out,) * 3 + (jax.ShapeDtypeStruct(table.shape, F32),)
    results = pl.pallas_call(
        functools.partial(kernel, dp_size),
        out_shape=shapes,
        in_specs=[hbm] * 5 + [smem, vmem] + [hbm] * 5 + [smem, vmem, vmem],
        out_specs=(hbm,) * 6 + (vmem,),
        scratch_shapes=[pltpu.VMEM((7 * span, wide), BF16)] * 4
        + [pltpu.VMEM((span, width), BF16)] * 2
        + [pltpu.VMEM((4, 8, 128), F32), pltpu.VMEM((3, 8, 128), F32), pltpu.VMEM((3, 8, 128), F32)]
        + [pltpu.VMEM((rows, width), BF16)] * 8
        + [pltpu.VMEM((4 * span, wide), BF16)] * 3
        + [pltpu.VMEM((4 * span, wide), F32)] * 3
        + [pltpu.VMEM((7 * span, wide), F32), pltpu.VMEM((4 * 2 * WIN * span, span), F32)]
        + [pltpu.VMEM((8, 128), F32), pltpu.VMEM((128, 128), F32), pltpu.VMEM((2, 16, 8, 128), F32)]
        + [
            dma((11,)), dma((4, 4)), dma((4, 4)), dma((3,)), dma((3,)), dma((4, 3)), dma((4, 3)),
            dma((3,)), dma((3,)), dma((3, 4)), dma((3, 4)), dma((3,)), dma((2, 15)), dma((2, 15)), dma((3,)),
        ],
        compiler_params=pltpu.CompilerParams(
            collective_id=0, has_side_effects=True, vmem_limit_bytes=VMEM_LIMIT
        ),
        name="window_grads",
    )(q, k, v, o, g, groups, gap_long, qs, ks, vs, os, gs, lengths, gap_short.reshape(1, -1), table)
    return pl.pallas_call(
        place_kernel,
        out_shape=shapes,
        in_specs=[hbm] * 7,
        out_specs=(hbm,) * 7,
        scratch_shapes=[pltpu.VMEM(shape.shape, shape.dtype) for shape in shapes] + [dma((7,)), dma((7,))],
        compiler_params=pltpu.CompilerParams(vmem_limit_bytes=VMEM_LIMIT),
        name="place",
    )(*results)


def solution(mesh):
    placed = (
        (P("dp", "blk", None),) * 5
        + (P("dp", None), P("dp", None))
        + (P(("dp", "blk"), None),) * 5
        + (P(("dp", "blk")), P(("dp", "blk")), P())
    )
    return jax.shard_map(
        functools.partial(body, mesh.shape["dp"]),
        mesh=mesh,
        in_specs=placed,
        out_specs=(P("dp", "blk", None),) * 3 + (P(("dp", "blk"), None),) * 3 + (P(),),
        check_vma=False,
    )
```

```python
import functools
import math

import jax
import jax.numpy as jnp
from jax import lax
from jax.experimental import pallas as pl
from jax.experimental.pallas import tpu as pltpu
from jax.sharding import PartitionSpec as P

NEG = -1e30
LOG2E = math.log2(math.e)
MESH = pl.DeviceIdType.MESH
RING = 4
WIN = 4
Q, G, K, V = 0, 1, 2, 3
F32 = jnp.float32
VMEM_LIMIT = 56 * 1024 * 1024
BF16 = jnp.bfloat16


def dot_nn(a, b):
    return lax.dot_general(a, b, (((1,), (0,)), ((), ())), preferred_element_type=F32)


def dot_nt(a, b):
    return lax.dot_general(a, b, (((1,), (1,)), ((), ())), preferred_element_type=F32)


def dot_tn(a, b):
    return lax.dot_general(a, b, (((0,), (0,)), ((), ())), preferred_element_type=F32)


def halves(value):
    high = value.astype(BF16)
    return high, (value - high.astype(F32)).astype(BF16)


def row_pick(row, count=8, width=128):
    rows = lax.broadcasted_iota(jnp.int32, (count, width), 0)
    return jnp.where(rows == row, 1.0, 0.0).astype(BF16)


def lane_sums(value, row):
    pick = row_pick(row)
    high, low = halves(value)
    return dot_nt(pick, high) + dot_nt(pick, low)


def bucket_sums(column, onehot):
    high, low = halves(column)
    return dot_nt(high, onehot) + dot_nt(low, onehot)


def place_kernel(*refs):
    count = (len(refs) - 2) // 3
    ins, outs, held = refs[:count], refs[count : 2 * count], refs[2 * count : 3 * count]
    in_sem, out_sem = refs[3 * count :]
    loads = [pltpu.make_async_copy(ins[n], held[n], in_sem.at[n]) for n in range(count)]
    stores = [pltpu.make_async_copy(held[n], outs[n], out_sem.at[n]) for n in range(count)]
    for copy in loads:
        copy.start()
    for load, store in zip(loads, stores):
        load.wait()
        store.start()
    for copy in stores:
        copy.wait()


def kernel(
    dp_size,
    q_ref, k_ref, v_ref, o_ref, g_ref, group_ref, gap_ref,
    qs_ref, ks_ref, vs_ref, os_ref, gs_ref, len_ref, gaps_ref, table_ref,
    gq_ref, gk_ref, gv_ref, gqs_ref, gks_ref, gvs_ref, gb_ref,
    qb, gb, kb, vb, g_own, o_own, delta_buf, stat_out, stat_in,
    qs, ks, vs, os, gs, dqs, dks, dvs,
    dq_out, dk_out, dv_out, bias_sum, probs_buf, plow_buf, dlow_buf,
    bias_rows, bias_cols, reduce_buf,
    load_sem, a2a_send, a2a_recv, delta_send, delta_recv, z_send, z_recv,
    stat_send, stat_recv, out_send, out_recv, own_sem, red_send, red_recv, store_sem,
):
    dp = lax.axis_index("dp")
    blk = lax.axis_index("blk")
    x = blk % RING
    z = blk // RING
    planes = 4
    span = 128
    depth = 128
    heads = table_ref.shape[0]
    mine = heads // RING
    wide = mine * depth
    scale = depth ** (-0.5)
    score_scale = scale * LOG2E
    halo = WIN - 1

    bufs = (qb, gb, kb, vb)
    ins = (q_ref, g_ref, k_ref, v_ref)
    base = (0, 0, halo, halo)

    def rows(n):
        if isinstance(n, int):
            return pl.ds(n * span, span)
        return pl.ds(pl.multiple_of(n * span, span), span)

    def at(zz, xx):
        return (dp, zz * RING + xx)

    up, down = (z + 1) % planes, (z + planes - 1) % planes

    y, c4 = (dp // 4, dp % 4) if dp_size > 1 else (0, 0)
    y_size, c_size = (4, 4) if dp_size > 1 else (1, 1)

    def across_plane(dy, dx):
        yy, xx = (y + dy) % y_size, (x + dx) % RING
        return (yy * 4 + c4, z * RING + xx), yy * RING + xx

    def across_planes(dz, dc):
        zz, cc = (z + dz) % planes, (c4 + dc) % c_size
        return (y * 4 + cc, zz * RING + x), zz * c_size + cc

    stages = [
        (y * RING + x, y_size * RING, [across_plane(a, b)[0] for a in range(y_size) for b in range(RING) if a or b]),
        (z * c_size + c4, planes * c_size, [across_planes(a, b)[0] for a in range(planes) for b in range(c_size) if a or b]),
    ]
    peers = stages[0][2] + stages[1][2]

    def own_cols(ref, xx):
        return ref.at[0, :, pl.ds(pl.multiple_of(xx * wide, wide), wide)]

    def a2a(t, to):
        return pltpu.make_async_remote_copy(
            src_ref=own_cols(ins[t], to),
            dst_ref=bufs[t].at[rows(base[t] + x)],
            send_sem=a2a_send.at[t, to], recv_sem=a2a_recv.at[t, x],
            device_id=at(z, to), device_id_type=MESH,
        )

    def a2a_arrival(t, source):
        return pltpu.make_async_remote_copy(
            src_ref=own_cols(ins[t], source),
            dst_ref=bufs[t].at[rows(base[t] + source)],
            send_sem=a2a_send.at[t, source], recv_sem=a2a_recv.at[t, source],
            device_id=at(z, source), device_id_type=MESH,
        )

    def own_load(t):
        return pltpu.make_async_copy(own_cols(ins[t], x), bufs[t].at[rows(base[t] + x)], load_sem.at[t])

    def across(t, c, own):
        src = own_cols(ins[t], x) if own else bufs[t].at[rows(base[t] + c)]
        if t in (Q, G):
            slot, index, to = RING + c, c, down
        else:
            slot, index, to = c - 1, c - 1, up
        return pltpu.make_async_remote_copy(
            src_ref=src, dst_ref=bufs[t].at[rows(slot)],
            send_sem=z_send.at[t, index], recv_sem=z_recv.at[t, index],
            device_id=at(to, x), device_id_type=MESH,
        )

    def crosses(t, c):
        return c <= halo - 1 if t in (Q, G) else c >= 1

    def delta_copy(r):
        return pltpu.make_async_remote_copy(
            src_ref=delta_buf.at[x], dst_ref=delta_buf.at[x],
            send_sem=delta_send.at[r - 1], recv_sem=delta_recv.at[r - 1],
            device_id=at(z, (x + r) % RING), device_id_type=MESH,
        )

    def stat_copy(c):
        return pltpu.make_async_remote_copy(
            src_ref=stat_out.at[c], dst_ref=stat_in.at[c],
            send_sem=stat_send.at[c], recv_sem=stat_recv.at[c],
            device_id=at(down, x), device_id_type=MESH,
        )

    stage_bufs = (dq_out, dk_out, dv_out)
    outs = (gq_ref, gk_ref, gv_ref)

    def out_copy(t, c):
        return pltpu.make_async_remote_copy(
            src_ref=stage_bufs[t].at[rows(c)], dst_ref=own_cols(outs[t], x),
            send_sem=out_send.at[t, c], recv_sem=out_recv.at[t, x],
            device_id=at(z, c), device_id_type=MESH,
        )

    def out_arrival(t, r):
        source = (x + r) % RING
        return pltpu.make_async_remote_copy(
            src_ref=stage_bufs[t].at[rows(0)], dst_ref=own_cols(outs[t], source),
            send_sem=out_send.at[t, 0], recv_sem=out_recv.at[t, source],
            device_id=at(z, source), device_id_type=MESH,
        )

    def out_own(t, c):
        return pltpu.make_async_copy(stage_bufs[t].at[rows(c)], own_cols(outs[t], x), own_sem.at[t])

    def send_out(t, c):
        @pl.when(x == c)
        def _():
            out_own(t, c).start()

        @pl.when(x != c)
        def _():
            out_copy(t, c).start()

    loads = [own_load(t) for t in range(4)]
    loads.append(pltpu.make_async_copy(g_ref.at[0], g_own, load_sem.at[4]))
    loads.append(pltpu.make_async_copy(o_ref.at[0], o_own, load_sem.at[5]))
    short_loads = [
        pltpu.make_async_copy(src, dst, load_sem.at[6 + n])
        for n, (src, dst) in enumerate(
            ((qs_ref, qs), (ks_ref, ks), (vs_ref, vs), (os_ref, os), (gs_ref, gs))
        )
    ]
    for copy in loads[4:] + short_loads + loads[:4]:
        copy.start()

    barrier = pltpu.get_barrier_semaphore()
    for peer in peers:
        pl.semaphore_signal(barrier, inc=1, device_id=peer, device_id_type=MESH)
    pl.semaphore_wait(barrier, len(peers))

    order = (1, 3, 2)
    def across_own(t, condition):
        @pl.when(condition)
        def _():
            across(t, x, True).start()

    for t in (K, Q):
        across_own(t, crosses(t, x))

    for first, second in ((K, Q), (V, G)):
        for n in range(RING):
            for t, to in ((first, n), (second, RING - 1 - n)):

                @pl.when(x != to)
                def _(t=t, to=to):
                    a2a(t, to).start()

    loads[4].wait()
    loads[5].wait()
    delta = jnp.zeros((8, span), F32)
    for h in range(heads):
        cols = pl.ds(h * depth, depth)
        delta = delta + lane_sums(g_own[:, cols].astype(F32) * o_own[:, cols].astype(F32), h)
    delta_buf[x] = delta
    for r in order:
        delta_copy(r).start()

    table = table_ref[...] * LOG2E
    buckets = lax.broadcasted_iota(jnp.int32, (table.shape[1], span), 0)
    buckets_wide = lax.broadcasted_iota(jnp.int32, (128, span), 0)

    def bias_of(gaps):
        onehot = jnp.where(buckets == gaps, 1.0, 0.0)
        return jnp.dot(table, onehot, precision=lax.Precision.HIGHEST, preferred_element_type=F32)

    def long_gaps(n):
        shard = (z * RING + n - halo + 16) % 16
        return gap_ref[:, rows(shard)]

    bias_cols[...] = jnp.zeros((128, 128), F32)
    for n in range(halo + RING):
        bias_rows[...] = bias_of(long_gaps(n))
        for h in range(mine):
            bias_cols[pl.ds(n * mine + h, 1), :] = bias_rows[pl.ds(x * mine + h, 1), :]
    for b in range(2):
        bias_cols[pl.ds(16 + 8 * b, 8), :] = bias_of(gaps_ref[:, rows(b)])
    bias_cols[...] = bias_cols[...].T

    key_rows = lax.broadcasted_iota(jnp.int32, (span, span), 0)
    query_cols = lax.broadcasted_iota(jnp.int32, (span, span), 1)
    causal = key_rows <= query_cols

    for copy in short_loads:
        copy.wait()

    def short_step(step, columns):
        columns = list(columns)
        for b in range(2):
            length = len_ref[b]
            allowed = causal & (key_rows < length)
            live = lax.broadcasted_iota(jnp.int32, (1, span), 1) < length
            for inner in range(2):
                h = step * 2 + inner
                cols = pl.ds(h * depth, depth)
                r = rows(b)
                bias = jnp.sum(
                    jnp.where(query_cols == 16 + 8 * b + h, bias_cols[...], 0.0), axis=1, keepdims=True
                )
                query, keys, values, grad = qs[r, cols], ks[r, cols], vs[r, cols], gs[r, cols]
                prod = grad.astype(F32) * os[r, cols].astype(F32)
                delta = lane_sums(prod, 0)[0:1]
                scores = dot_nt(keys, query) * score_scale + bias
                scores = jnp.where(allowed, scores, NEG)
                top = jnp.max(scores, axis=0, keepdims=True)
                weights = jnp.exp2(scores - top)
                inverse = 1.0 / jnp.sum(weights, axis=0, keepdims=True)
                probs = weights * jnp.where(live, inverse, 0.0)
                dprobs = dot_nt(values, grad)
                dscores = probs * (dprobs - delta)
                dlow = dscores.astype(BF16)
                dqs[r, cols] = (dot_tn(dlow, keys) * scale).astype(BF16)
                dks[r, cols] = (dot_nn(dlow, query) * scale).astype(BF16)
                dvs[r, cols] = dot_nn(probs.astype(BF16), grad).astype(BF16)
                columns[b] = columns[b] + lane_sums(dscores, h)
        return tuple(columns)

    zero_col = jnp.zeros((8, span), F32)
    short_columns = (zero_col, zero_col)

    def arrive_here(t, c):
        @pl.when(x != c)
        def _():
            a2a_arrival(t, c).wait_recv()

    def onward(t, c):
        @pl.when(x != c)
        def _():
            across(t, c, False).start()

    def forward(t, c):
        arrive_here(t, c)
        onward(t, c)

    def forward_rest(up_tensor, down_tensor):
        arrive_here(up_tensor, 0)
        arrive_here(down_tensor, RING - 1)

    def arrive(t, c):
        across(t, c, False).wait_recv()

    def penalty(query_shard, key_shard):
        there = (query_shard < 16) & (key_shard >= 0)
        same = group_ref[0, (query_shard + 16) % 16] == group_ref[0, (key_shard + 16) % 16]
        return jnp.where(there & same, 0.0, NEG).astype(F32)

    def bias_col(n, h):
        return bias_cols[:, pl.ds(n * mine + h, 1)]

    def block(first, count=1):
        return pl.ds(first * span, count * span)

    def delta_row(c, h):
        return delta_buf[c, pl.ds(x * mine + h, 1), :]

    def stats(c):
        for h in range(mine):
            cols = pl.ds(h * depth, depth)
            products = dot_nt(kb[block(c, WIN), cols], qb[block(c), cols])
            scores = []
            for w in range(WIN):
                n = c + w
                pen = penalty(z * RING + c, z * RING + n - halo)
                s = products[w * span : (w + 1) * span] * score_scale + (bias_col(n, h) + pen)
                if w == WIN - 1:
                    s = jnp.where(causal, s, NEG)
                scores.append(s)
            top = scores[0]
            for s in scores[1:]:
                top = jnp.maximum(top, s)
            top = jnp.max(top, axis=0, keepdims=True)
            weights = [jnp.exp2(s - top) for s in scores]
            total = weights[0]
            for weight in weights[1:]:
                total = total + weight
            inverse = 1.0 / jnp.sum(total, axis=0, keepdims=True)
            for w in range(WIN):
                n = c + w
                probs = weights[w] * inverse
                probs_buf[h, block(n), block(c)] = probs
                if n >= halo:
                    plow_buf[h, block(n - halo), block(c)] = probs.astype(BF16)
            if c < halo:
                stat_out[c, pl.ds(h, 1), :] = top
                stat_out[c, pl.ds(2 + h, 1), :] = inverse
                stat_out[c, pl.ds(4 + h, 1), :] = delta_row(c, h)
        if c < halo:
            stat_copy(c).start()

    def key_row(n):
        low, high = max(0, n - halo), min(RING - 1, n)
        for h in range(mine):
            cols = pl.ds(h * depth, depth)
            dprobs = dot_nt(vb[block(n), cols], gb[block(low, high - low + 1), cols])
            column = None
            for c in range(low, high + 1):
                at_c = (c - low) * span
                dscores = probs_buf[h, block(n), block(c)] * (dprobs[:, at_c : at_c + span] - delta_row(c, h))
                dlow_buf[h, block(n), block(c)] = dscores.astype(BF16)
                column = dscores if column is None else column + dscores
            if n >= halo - 1:
                bias_sum[block(n), cols] = column

    def key_home(c):
        first, count = c + 1, RING - 1 - c
        for h in range(mine):
            cols = pl.ds(h * depth, depth)
            query, grad = qb[block(RING + c), cols], gb[block(RING + c), cols]
            top = stat_in[c, pl.ds(h, 1), :]
            inverse = stat_in[c, pl.ds(2 + h, 1), :]
            delta = stat_in[c, pl.ds(4 + h, 1), :]
            products = dot_nt(kb[block(first + halo, count), cols], query)
            dprobs = dot_nt(vb[block(first + halo, count), cols], grad)
            for k in range(first, RING):
                n = k + halo
                at_k = (k - first) * span
                pen = penalty((z + 1) * RING + c, z * RING + k)
                s = products[at_k : at_k + span] * score_scale + (bias_col(n, h) + pen)
                probs = jnp.exp2(s - top) * inverse
                dscores = probs * (dprobs[at_k : at_k + span] - delta)
                plow_buf[h, block(k), block(RING + c)] = probs.astype(BF16)
                dlow_buf[h, block(n), block(RING + c)] = dscores.astype(BF16)
                if k < RING - 1:
                    bias_sum[block(n), cols] += dscores

    def finish_query(c):
        for h in range(mine):
            cols = pl.ds(h * depth, depth)
            dquery = dot_tn(dlow_buf[h, block(c, WIN), block(c)], kb[block(c, WIN), cols])
            dq_out[block(c), cols] = (dquery * scale).astype(BF16)
        send_out(0, c)

    def finish(k):
        for h in range(mine):
            cols = pl.ds(h * depth, depth)
            dkey = dot_nn(dlow_buf[h, block(k + halo), block(k, WIN)], qb[block(k, WIN), cols])
            dk_out[block(k), cols] = (dkey * scale).astype(BF16)
        send_out(1, k)
        for h in range(mine):
            cols = pl.ds(h * depth, depth)
            dvalue = dot_nn(plow_buf[h, block(k), block(k, WIN)], gb[block(k, WIN), cols])
            dv_out[block(k), cols] = dvalue.astype(BF16)
        send_out(2, k)

    def reduce_copies(s):
        place, size, others = stages[s]
        return [
            pltpu.make_async_remote_copy(
                src_ref=reduce_buf.at[s, place], dst_ref=reduce_buf.at[s, place],
                send_sem=red_send.at[s, n], recv_sem=red_recv.at[s, n],
                device_id=other, device_id_type=MESH,
            )
            for n, other in enumerate(others)
        ]

    def reduce_start(s, value):
        reduce_buf[s, stages[s][0]] = value
        for copy in reduce_copies(s):
            copy.start()

    def reduce_end(s):
        for copy in reduce_copies(s):
            copy.wait_recv()
        value = reduce_buf[s, 0]
        for n in range(1, stages[s][1]):
            value = value + reduce_buf[s, n]
        return value

    short_columns = short_step(0, short_columns)
    forward(K, 3)
    forward(Q, 0)
    forward(K, 2)
    forward(Q, 1)
    short_columns = short_step(1, short_columns)
    forward(K, 1)
    forward(Q, 2)
    across_own(V, (x == 3) | (x == 2))
    across_own(G, (x == 0) | (x == 1))
    short_columns = short_step(2, short_columns)
    forward(V, 3)
    forward(G, 0)
    forward(V, 2)
    forward(G, 1)
    short_columns = short_step(3, short_columns)
    for copy in loads[:4]:
        copy.wait()
    for r in order:
        delta_copy(r).wait_recv()
    arrive_here(V, 1)
    arrive_here(G, 2)
    forward_rest(K, Q)
    forward_rest(V, G)
    stats(3)
    for c in (2, 1, 0):
        arrive(K, c + 1)
        stats(c)
    across(V, 3, False).wait_send()
    across(G, 0, False).wait_send()
    onward(V, 1)
    onward(G, 2)
    across_own(V, x == 1)
    across_own(G, x == 2)

    for n in range(halo, halo + RING):
        key_row(n)
    stores = [
        pltpu.make_async_copy(src, dst, store_sem.at[n])
        for n, (src, dst) in enumerate(((dqs, gqs_ref), (dks, gks_ref), (dvs, gvs_ref)))
    ]
    for copy in stores:
        copy.start()

    local_bias = jnp.zeros((8, 128), F32)
    for b in range(2):
        onehot = jnp.where(buckets_wide == gaps_ref[:, rows(b)], 1.0, 0.0).astype(BF16)
        local_bias = local_bias + bucket_sums(short_columns[b], onehot)

    arrive(V, 3)
    key_row(2)
    for c in (0, 1):
        arrive(Q, c)
        arrive(G, c)
        stat_copy(c).wait_recv()
        key_home(c)

    for n in range(halo - 1, halo + RING):
        onehot = jnp.where(buckets_wide == long_gaps(n), 1.0, 0.0).astype(BF16)
        column = zero_col
        for h in range(mine):
            column = column + lane_sums(bias_sum[block(n), pl.ds(h * depth, depth)], x * mine + h)
        local_bias = local_bias + bucket_sums(column, onehot)
    reduce_start(0, local_bias)

    finish_query(3)
    finish(0)
    finish_query(2)
    finish(1)
    finish(2)
    arrive(V, 2)
    key_row(1)
    finish_query(1)
    arrive(V, 1)
    key_row(0)
    finish_query(0)
    arrive(Q, 2)
    arrive(G, 2)
    stat_copy(2).wait_recv()
    key_home(2)
    finish(3)
    reduce_start(1, reduce_end(0))
    gb_ref[...] = reduce_end(1)[:, : gb_ref.shape[1]]

    for t in range(3):
        out_own(t, 0).wait()
        for c in range(RING):

            @pl.when(x != c)
            def _(t=t, c=c):
                out_copy(t, c).wait_send()

        for r in range(1, RING):
            out_arrival(t, r).wait_recv()
    for c in range(halo):
        stat_copy(c).wait_send()
    for r in order:
        delta_copy(r).wait_send()
    for s in range(2):
        for copy in reduce_copies(s):
            copy.wait_send()
    for t in range(4):
        for to in range(RING):

            @pl.when(x != to)
            def _(t=t, to=to):
                a2a(t, to).wait_send()

        for index in range(halo):
            c = index if t in (Q, G) else index + 1
            if (t, c) not in ((V, 3), (G, 0)):
                across(t, c, False).wait_send()
    for copy in stores:
        copy.wait()


def body(dp_size, q, k, v, o, g, groups, gap_long, qs, ks, vs, os, gs, lengths, gap_short, table):
    hbm = pl.BlockSpec(memory_space=pltpu.HBM)
    vmem = pl.BlockSpec(memory_space=pltpu.VMEM)
    smem = pl.BlockSpec(memory_space=pltpu.SMEM)
    span, width = q.shape[1:]
    rows = qs.shape[0]
    wide = width // RING
    dma = pltpu.SemaphoreType.DMA
    long_out = jax.ShapeDtypeStruct(q.shape, q.dtype)
    short_out = jax.ShapeDtypeStruct(qs.shape, qs.dtype)
    shapes = (long_out,) * 3 + (short_out,) * 3 + (jax.ShapeDtypeStruct(table.shape, F32),)
    results = pl.pallas_call(
        functools.partial(kernel, dp_size),
        out_shape=shapes,
        in_specs=[hbm] * 5 + [smem, vmem] + [hbm] * 5 + [smem, vmem, vmem],
        out_specs=(hbm,) * 6 + (vmem,),
        scratch_shapes=[pltpu.VMEM((7 * span, wide), BF16)] * 4
        + [pltpu.VMEM((span, width), BF16)] * 2
        + [pltpu.VMEM((4, 8, 128), F32), pltpu.VMEM((3, 8, 128), F32), pltpu.VMEM((3, 8, 128), F32)]
        + [pltpu.VMEM((rows, width), BF16)] * 8
        + [pltpu.VMEM((4 * span, wide), BF16)] * 3
        + [pltpu.VMEM((7 * span, wide), F32), pltpu.VMEM((2, 7 * span, 4 * span), F32)]
        + [pltpu.VMEM((2, 4 * span, 7 * span), BF16), pltpu.VMEM((2, 7 * span, 7 * span), BF16)]
        + [pltpu.VMEM((8, 128), F32), pltpu.VMEM((128, 128), F32), pltpu.VMEM((2, 16, 8, 128), F32)]
        + [
            dma((11,)), dma((4, 4)), dma((4, 4)), dma((3,)), dma((3,)), dma((4, 3)), dma((4, 3)),
            dma((3,)), dma((3,)), dma((3, 4)), dma((3, 4)), dma((3,)), dma((2, 15)), dma((2, 15)), dma((3,)),
        ],
        compiler_params=pltpu.CompilerParams(
            collective_id=0, has_side_effects=True, vmem_limit_bytes=VMEM_LIMIT
        ),
        name="window_grads",
    )(q, k, v, o, g, groups, gap_long, qs, ks, vs, os, gs, lengths, gap_short.reshape(1, -1), table)
    return pl.pallas_call(
        place_kernel,
        out_shape=shapes,
        in_specs=[hbm] * 7,
        out_specs=(hbm,) * 7,
        scratch_shapes=[pltpu.VMEM(shape.shape, shape.dtype) for shape in shapes] + [dma((7,)), dma((7,))],
        compiler_params=pltpu.CompilerParams(vmem_limit_bytes=VMEM_LIMIT),
        name="place",
    )(*results)


def solution(mesh):
    placed = (
        (P("dp", "blk", None),) * 5
        + (P("dp", None), P("dp", None))
        + (P(("dp", "blk"), None),) * 5
        + (P(("dp", "blk")), P(("dp", "blk")), P())
    )
    return jax.shard_map(
        functools.partial(body, mesh.shape["dp"]),
        mesh=mesh,
        in_specs=placed,
        out_specs=(P("dp", "blk", None),) * 3 + (P(("dp", "blk"), None),) * 3 + (P(),),
        check_vma=False,
    )
```

```python
import functools
import math

import jax
import jax.numpy as jnp
from jax import lax
from jax.experimental import pallas as pl
from jax.experimental.pallas import tpu as pltpu
from jax.sharding import PartitionSpec as P

NEG = -1e30
LOG2E = math.log2(math.e)
MESH = pl.DeviceIdType.MESH
RING = 4
WIN = 4
Q, G, K, V = 0, 1, 2, 3
F32 = jnp.float32
VMEM_LIMIT = 56 * 1024 * 1024
BF16 = jnp.bfloat16


def dot_nn(a, b):
    return lax.dot_general(a, b, (((1,), (0,)), ((), ())), preferred_element_type=F32)


def dot_nt(a, b):
    return lax.dot_general(a, b, (((1,), (1,)), ((), ())), preferred_element_type=F32)


def dot_tn(a, b):
    return lax.dot_general(a, b, (((0,), (0,)), ((), ())), preferred_element_type=F32)


def halves(value):
    high = value.astype(BF16)
    return high, (value - high.astype(F32)).astype(BF16)


def row_pick(row, count=8, width=128):
    rows = lax.broadcasted_iota(jnp.int32, (count, width), 0)
    return jnp.where(rows == row, 1.0, 0.0).astype(BF16)


def lane_sums(value, row):
    pick = row_pick(row)
    high, low = halves(value)
    return dot_nt(pick, high) + dot_nt(pick, low)


def bucket_sums(column, onehot):
    high, low = halves(column)
    return dot_nt(high, onehot) + dot_nt(low, onehot)


def place_kernel(*refs):
    count = (len(refs) - 2) // 3
    ins, outs, held = refs[:count], refs[count : 2 * count], refs[2 * count : 3 * count]
    in_sem, out_sem = refs[3 * count :]
    loads = [pltpu.make_async_copy(ins[n], held[n], in_sem.at[n]) for n in range(count)]
    stores = [pltpu.make_async_copy(held[n], outs[n], out_sem.at[n]) for n in range(count)]
    for copy in loads:
        copy.start()
    for load, store in zip(loads, stores):
        load.wait()
        store.start()
    for copy in stores:
        copy.wait()


def kernel(
    dp_size,
    q_ref, k_ref, v_ref, o_ref, g_ref, group_ref, gap_ref,
    qs_ref, ks_ref, vs_ref, os_ref, gs_ref, len_ref, gaps_ref, table_ref,
    gq_ref, gk_ref, gv_ref, gqs_ref, gks_ref, gvs_ref, gb_ref,
    qb, gb, kb, vb, g_own, o_own, delta_buf, stat_out, stat_in,
    qs, ks, vs, os, gs, dqs, dks, dvs,
    dq_out, dk_out, dv_out, bias_sum, probs_buf, plow_buf, dlow_buf,
    bias_rows, bias_cols, reduce_buf,
    load_sem, a2a_send, a2a_recv, delta_send, delta_recv, z_send, z_recv,
    stat_send, stat_recv, out_send, out_recv, own_sem, red_send, red_recv, store_sem,
):
    dp = lax.axis_index("dp")
    blk = lax.axis_index("blk")
    x = blk % RING
    z = blk // RING
    planes = 4
    span = 128
    depth = 128
    heads = table_ref.shape[0]
    mine = heads // RING
    wide = mine * depth
    scale = depth ** (-0.5)
    score_scale = scale * LOG2E
    halo = WIN - 1

    bufs = (qb, gb, kb, vb)
    ins = (q_ref, g_ref, k_ref, v_ref)
    base = (0, 0, halo, halo)

    def rows(n):
        if isinstance(n, int):
            return pl.ds(n * span, span)
        return pl.ds(pl.multiple_of(n * span, span), span)

    def at(zz, xx):
        return (dp, zz * RING + xx)

    up, down = (z + 1) % planes, (z + planes - 1) % planes

    y, c4 = (dp // 4, dp % 4) if dp_size > 1 else (0, 0)
    y_size, c_size = (4, 4) if dp_size > 1 else (1, 1)

    def across_plane(dy, dx):
        yy, xx = (y + dy) % y_size, (x + dx) % RING
        return (yy * 4 + c4, z * RING + xx), yy * RING + xx

    def across_planes(dz, dc):
        zz, cc = (z + dz) % planes, (c4 + dc) % c_size
        return (y * 4 + cc, zz * RING + x), zz * c_size + cc

    stages = [
        (y * RING + x, y_size * RING, [across_plane(a, b)[0] for a in range(y_size) for b in range(RING) if a or b]),
        (z * c_size + c4, planes * c_size, [across_planes(a, b)[0] for a in range(planes) for b in range(c_size) if a or b]),
    ]
    peers = stages[0][2] + stages[1][2]

    def own_cols(ref, xx):
        return ref.at[0, :, pl.ds(pl.multiple_of(xx * wide, wide), wide)]

    def a2a(t, to):
        return pltpu.make_async_remote_copy(
            src_ref=own_cols(ins[t], to),
            dst_ref=bufs[t].at[rows(base[t] + x)],
            send_sem=a2a_send.at[t, to], recv_sem=a2a_recv.at[t, x],
            device_id=at(z, to), device_id_type=MESH,
        )

    def a2a_arrival(t, source):
        return pltpu.make_async_remote_copy(
            src_ref=own_cols(ins[t], source),
            dst_ref=bufs[t].at[rows(base[t] + source)],
            send_sem=a2a_send.at[t, source], recv_sem=a2a_recv.at[t, source],
            device_id=at(z, source), device_id_type=MESH,
        )

    def own_load(t):
        return pltpu.make_async_copy(own_cols(ins[t], x), bufs[t].at[rows(base[t] + x)], load_sem.at[t])

    def across(t, c, own):
        src = own_cols(ins[t], x) if own else bufs[t].at[rows(base[t] + c)]
        if t in (Q, G):
            slot, index, to = RING + c, c, down
        else:
            slot, index, to = c - 1, c - 1, up
        return pltpu.make_async_remote_copy(
            src_ref=src, dst_ref=bufs[t].at[rows(slot)],
            send_sem=z_send.at[t, index], recv_sem=z_recv.at[t, index],
            device_id=at(to, x), device_id_type=MESH,
        )

    def crosses(t, c):
        return c <= halo - 1 if t in (Q, G) else c >= 1

    def delta_copy(r):
        return pltpu.make_async_remote_copy(
            src_ref=delta_buf.at[x], dst_ref=delta_buf.at[x],
            send_sem=delta_send.at[r - 1], recv_sem=delta_recv.at[r - 1],
            device_id=at(z, (x + r) % RING), device_id_type=MESH,
        )

    def stat_copy(c):
        return pltpu.make_async_remote_copy(
            src_ref=stat_out.at[c], dst_ref=stat_in.at[c],
            send_sem=stat_send.at[c], recv_sem=stat_recv.at[c],
            device_id=at(down, x), device_id_type=MESH,
        )

    stage_bufs = (dq_out, dk_out, dv_out)
    outs = (gq_ref, gk_ref, gv_ref)

    def out_copy(t, c):
        return pltpu.make_async_remote_copy(
            src_ref=stage_bufs[t].at[rows(c)], dst_ref=own_cols(outs[t], x),
            send_sem=out_send.at[t, c], recv_sem=out_recv.at[t, x],
            device_id=at(z, c), device_id_type=MESH,
        )

    def out_arrival(t, r):
        source = (x + r) % RING
        return pltpu.make_async_remote_copy(
            src_ref=stage_bufs[t].at[rows(0)], dst_ref=own_cols(outs[t], source),
            send_sem=out_send.at[t, 0], recv_sem=out_recv.at[t, source],
            device_id=at(z, source), device_id_type=MESH,
        )

    def out_own(t, c):
        return pltpu.make_async_copy(stage_bufs[t].at[rows(c)], own_cols(outs[t], x), own_sem.at[t])

    def send_out(t, c):
        @pl.when(x == c)
        def _():
            out_own(t, c).start()

        @pl.when(x != c)
        def _():
            out_copy(t, c).start()

    barrier = pltpu.get_barrier_semaphore()
    for peer in peers:
        pl.semaphore_signal(barrier, inc=1, device_id=peer, device_id_type=MESH)

    loads = [own_load(t) for t in range(4)]
    loads.append(pltpu.make_async_copy(g_ref.at[0], g_own, load_sem.at[4]))
    loads.append(pltpu.make_async_copy(o_ref.at[0], o_own, load_sem.at[5]))
    short_loads = [
        pltpu.make_async_copy(src, dst, load_sem.at[6 + n])
        for n, (src, dst) in enumerate(
            ((qs_ref, qs), (ks_ref, ks), (vs_ref, vs), (os_ref, os), (gs_ref, gs))
        )
    ]
    for copy in loads[4:]:
        copy.start()

    pl.semaphore_wait(barrier, len(peers))

    order = (1, 3, 2)
    def across_own(t, condition):
        @pl.when(condition)
        def _():
            across(t, x, True).start()

    for first, second in ((K, Q), (V, G)):
        for n in range(RING):
            for t, to in ((first, n), (second, RING - 1 - n)):

                @pl.when(x != to)
                def _(t=t, to=to):
                    a2a(t, to).start()

            if first == K and n == 0:
                for t in (K, Q):
                    across_own(t, crosses(t, x))

    for copy in short_loads + loads[:4]:
        copy.start()

    loads[4].wait()
    loads[5].wait()
    delta = jnp.zeros((8, span), F32)
    for h in range(heads):
        cols = pl.ds(h * depth, depth)
        delta = delta + lane_sums(g_own[:, cols].astype(F32) * o_own[:, cols].astype(F32), h)
    delta_buf[x] = delta
    for r in order:
        delta_copy(r).start()

    table = table_ref[...] * LOG2E
    buckets = lax.broadcasted_iota(jnp.int32, (table.shape[1], span), 0)
    buckets_wide = lax.broadcasted_iota(jnp.int32, (128, span), 0)

    def bias_of(gaps):
        onehot = jnp.where(buckets == gaps, 1.0, 0.0)
        return jnp.dot(table, onehot, precision=lax.Precision.HIGHEST, preferred_element_type=F32)

    def long_gaps(n):
        shard = (z * RING + n - halo + 16) % 16
        return gap_ref[:, rows(shard)]

    bias_cols[...] = jnp.zeros((128, 128), F32)
    for n in range(halo + RING):
        bias_rows[...] = bias_of(long_gaps(n))
        for h in range(mine):
            bias_cols[pl.ds(n * mine + h, 1), :] = bias_rows[pl.ds(x * mine + h, 1), :]
    for b in range(2):
        bias_cols[pl.ds(16 + 8 * b, 8), :] = bias_of(gaps_ref[:, rows(b)])
    bias_cols[...] = bias_cols[...].T

    key_rows = lax.broadcasted_iota(jnp.int32, (span, span), 0)
    query_cols = lax.broadcasted_iota(jnp.int32, (span, span), 1)
    causal = key_rows <= query_cols

    for copy in short_loads:
        copy.wait()

    def short_step(step, columns):
        columns = list(columns)
        for b in range(2):
            length = len_ref[b]
            allowed = causal & (key_rows < length)
            live = lax.broadcasted_iota(jnp.int32, (1, span), 1) < length
            for inner in range(2):
                h = step * 2 + inner
                cols = pl.ds(h * depth, depth)
                r = rows(b)
                bias = jnp.sum(
                    jnp.where(query_cols == 16 + 8 * b + h, bias_cols[...], 0.0), axis=1, keepdims=True
                )
                query, keys, values, grad = qs[r, cols], ks[r, cols], vs[r, cols], gs[r, cols]
                prod = grad.astype(F32) * os[r, cols].astype(F32)
                delta = lane_sums(prod, 0)[0:1]
                scores = dot_nt(keys, query) * score_scale + bias
                scores = jnp.where(allowed, scores, NEG)
                top = jnp.max(scores, axis=0, keepdims=True)
                weights = jnp.exp2(scores - top)
                inverse = 1.0 / jnp.sum(weights, axis=0, keepdims=True)
                probs = weights * jnp.where(live, inverse, 0.0)
                dprobs = dot_nt(values, grad)
                dscores = probs * (dprobs - delta)
                dlow = dscores.astype(BF16)
                dqs[r, cols] = (dot_tn(dlow, keys) * scale).astype(BF16)
                dks[r, cols] = (dot_nn(dlow, query) * scale).astype(BF16)
                dvs[r, cols] = dot_nn(probs.astype(BF16), grad).astype(BF16)
                columns[b] = columns[b] + lane_sums(dscores, h)
        return tuple(columns)

    zero_col = jnp.zeros((8, span), F32)
    short_columns = (zero_col, zero_col)

    def arrive_here(t, c):
        @pl.when(x != c)
        def _():
            a2a_arrival(t, c).wait_recv()

    def onward(t, c):
        @pl.when(x != c)
        def _():
            across(t, c, False).start()

    def forward(t, c):
        arrive_here(t, c)
        onward(t, c)

    def forward_rest(up_tensor, down_tensor):
        arrive_here(up_tensor, 0)
        arrive_here(down_tensor, RING - 1)

    def arrive(t, c):
        across(t, c, False).wait_recv()

    def penalty(query_shard, key_shard):
        there = (query_shard < 16) & (key_shard >= 0)
        same = group_ref[0, (query_shard + 16) % 16] == group_ref[0, (key_shard + 16) % 16]
        return jnp.where(there & same, 0.0, NEG).astype(F32)

    def bias_col(n, h):
        return bias_cols[:, pl.ds(n * mine + h, 1)]

    def block(first, count=1):
        return pl.ds(first * span, count * span)

    def delta_row(c, h):
        return delta_buf[c, pl.ds(x * mine + h, 1), :]

    def stats(c):
        for h in range(mine):
            cols = pl.ds(h * depth, depth)
            products = dot_nt(kb[block(c, WIN), cols], qb[block(c), cols])
            scores = []
            for w in range(WIN):
                n = c + w
                pen = penalty(z * RING + c, z * RING + n - halo)
                s = products[w * span : (w + 1) * span] * score_scale + (bias_col(n, h) + pen)
                if w == WIN - 1:
                    s = jnp.where(causal, s, NEG)
                scores.append(s)
            top = scores[0]
            for s in scores[1:]:
                top = jnp.maximum(top, s)
            top = jnp.max(top, axis=0, keepdims=True)
            weights = [jnp.exp2(s - top) for s in scores]
            total = weights[0]
            for weight in weights[1:]:
                total = total + weight
            inverse = 1.0 / jnp.sum(total, axis=0, keepdims=True)
            for w in range(WIN):
                n = c + w
                probs = weights[w] * inverse
                probs_buf[h, block(n), block(c)] = probs
                if n >= halo:
                    plow_buf[h, block(n - halo), block(c)] = probs.astype(BF16)
            if c < halo:
                stat_out[c, pl.ds(h, 1), :] = top
                stat_out[c, pl.ds(2 + h, 1), :] = inverse
                stat_out[c, pl.ds(4 + h, 1), :] = delta_row(c, h)
        if c < halo:
            stat_copy(c).start()

    def key_row(n):
        low, high = max(0, n - halo), min(RING - 1, n)
        for h in range(mine):
            cols = pl.ds(h * depth, depth)
            dprobs = dot_nt(vb[block(n), cols], gb[block(low, high - low + 1), cols])
            column = None
            for c in range(low, high + 1):
                at_c = (c - low) * span
                dscores = probs_buf[h, block(n), block(c)] * (dprobs[:, at_c : at_c + span] - delta_row(c, h))
                dlow_buf[h, block(n), block(c)] = dscores.astype(BF16)
                column = dscores if column is None else column + dscores
            if n >= halo - 1:
                bias_sum[block(n), cols] = column

    def key_home(c):
        first, count = c + 1, RING - 1 - c
        for h in range(mine):
            cols = pl.ds(h * depth, depth)
            query, grad = qb[block(RING + c), cols], gb[block(RING + c), cols]
            top = stat_in[c, pl.ds(h, 1), :]
            inverse = stat_in[c, pl.ds(2 + h, 1), :]
            delta = stat_in[c, pl.ds(4 + h, 1), :]
            products = dot_nt(kb[block(first + halo, count), cols], query)
            dprobs = dot_nt(vb[block(first + halo, count), cols], grad)
            for k in range(first, RING):
                n = k + halo
                at_k = (k - first) * span
                pen = penalty((z + 1) * RING + c, z * RING + k)
                s = products[at_k : at_k + span] * score_scale + (bias_col(n, h) + pen)
                probs = jnp.exp2(s - top) * inverse
                dscores = probs * (dprobs[at_k : at_k + span] - delta)
                plow_buf[h, block(k), block(RING + c)] = probs.astype(BF16)
                dlow_buf[h, block(n), block(RING + c)] = dscores.astype(BF16)
                if k < RING - 1:
                    bias_sum[block(n), cols] += dscores

    def finish_query(c):
        for h in range(mine):
            cols = pl.ds(h * depth, depth)
            dquery = dot_tn(dlow_buf[h, block(c, WIN), block(c)], kb[block(c, WIN), cols])
            dq_out[block(c), cols] = (dquery * scale).astype(BF16)
        send_out(0, c)

    def finish(k):
        for h in range(mine):
            cols = pl.ds(h * depth, depth)
            dkey = dot_nn(dlow_buf[h, block(k + halo), block(k, WIN)], qb[block(k, WIN), cols])
            dk_out[block(k), cols] = (dkey * scale).astype(BF16)
        send_out(1, k)
        for h in range(mine):
            cols = pl.ds(h * depth, depth)
            dvalue = dot_nn(plow_buf[h, block(k), block(k, WIN)], gb[block(k, WIN), cols])
            dv_out[block(k), cols] = dvalue.astype(BF16)
        send_out(2, k)

    def reduce_copies(s):
        place, size, others = stages[s]
        return [
            pltpu.make_async_remote_copy(
                src_ref=reduce_buf.at[s, place], dst_ref=reduce_buf.at[s, place],
                send_sem=red_send.at[s, n], recv_sem=red_recv.at[s, n],
                device_id=other, device_id_type=MESH,
            )
            for n, other in enumerate(others)
        ]

    def reduce_start(s, value):
        reduce_buf[s, stages[s][0]] = value
        for copy in reduce_copies(s):
            copy.start()

    def reduce_end(s):
        for copy in reduce_copies(s):
            copy.wait_recv()
        value = reduce_buf[s, 0]
        for n in range(1, stages[s][1]):
            value = value + reduce_buf[s, n]
        return value

    short_columns = short_step(0, short_columns)
    forward(K, 3)
    forward(Q, 0)
    forward(K, 2)
    forward(Q, 1)
    short_columns = short_step(1, short_columns)
    forward(K, 1)
    forward(Q, 2)
    across_own(V, (x == 3) | (x == 2))
    across_own(G, (x == 0) | (x == 1))
    short_columns = short_step(2, short_columns)
    forward(V, 3)
    forward(G, 0)
    forward(V, 2)
    forward(G, 1)
    short_columns = short_step(3, short_columns)
    for copy in loads[:4]:
        copy.wait()
    for r in order:
        delta_copy(r).wait_recv()
    arrive_here(V, 1)
    arrive_here(G, 2)
    forward_rest(K, Q)
    forward_rest(V, G)
    stats(3)
    for c in (2, 1, 0):
        arrive(K, c + 1)
        stats(c)
    for n in range(halo, halo + RING):
        key_row(n)
    across(V, 3, False).wait_send()
    across(G, 0, False).wait_send()
    onward(V, 1)
    onward(G, 2)
    across_own(V, x == 1)
    across_own(G, x == 2)

    stores = [
        pltpu.make_async_copy(src, dst, store_sem.at[n])
        for n, (src, dst) in enumerate(((dqs, gqs_ref), (dks, gks_ref), (dvs, gvs_ref)))
    ]
    for copy in stores:
        copy.start()

    local_bias = jnp.zeros((8, 128), F32)
    for b in range(2):
        onehot = jnp.where(buckets_wide == gaps_ref[:, rows(b)], 1.0, 0.0).astype(BF16)
        local_bias = local_bias + bucket_sums(short_columns[b], onehot)

    arrive(V, 3)
    key_row(2)
    for c in (0, 1):
        arrive(Q, c)
        arrive(G, c)
        stat_copy(c).wait_recv()
        key_home(c)

    for n in range(halo - 1, halo + RING):
        onehot = jnp.where(buckets_wide == long_gaps(n), 1.0, 0.0).astype(BF16)
        column = zero_col
        for h in range(mine):
            column = column + lane_sums(bias_sum[block(n), pl.ds(h * depth, depth)], x * mine + h)
        local_bias = local_bias + bucket_sums(column, onehot)
    reduce_start(0, local_bias)

    finish_query(3)
    finish(0)
    finish_query(2)
    finish(1)
    finish(2)
    arrive(V, 2)
    key_row(1)
    finish_query(1)
    arrive(V, 1)
    key_row(0)
    finish_query(0)
    arrive(Q, 2)
    arrive(G, 2)
    stat_copy(2).wait_recv()
    key_home(2)
    finish(3)
    reduce_start(1, reduce_end(0))

    for t in range(3):
        out_own(t, 0).wait()
        for c in range(RING):

            @pl.when(x != c)
            def _(t=t, c=c):
                out_copy(t, c).wait_send()

        for r in range(1, RING):
            out_arrival(t, r).wait_recv()
    for c in range(halo):
        stat_copy(c).wait_send()
    for r in order:
        delta_copy(r).wait_send()
    for copy in reduce_copies(0):
        copy.wait_send()
    for t in range(4):
        for to in range(RING):

            @pl.when(x != to)
            def _(t=t, to=to):
                a2a(t, to).wait_send()

        for index in range(halo):
            c = index if t in (Q, G) else index + 1
            if (t, c) not in ((V, 3), (G, 0)):
                across(t, c, False).wait_send()
    for copy in stores:
        copy.wait()
    gb_ref[...] = reduce_end(1)[:, : gb_ref.shape[1]]
    for copy in reduce_copies(1):
        copy.wait_send()


def body(dp_size, q, k, v, o, g, groups, gap_long, qs, ks, vs, os, gs, lengths, gap_short, table):
    hbm = pl.BlockSpec(memory_space=pltpu.HBM)
    vmem = pl.BlockSpec(memory_space=pltpu.VMEM)
    smem = pl.BlockSpec(memory_space=pltpu.SMEM)
    span, width = q.shape[1:]
    rows = qs.shape[0]
    wide = width // RING
    dma = pltpu.SemaphoreType.DMA
    long_out = jax.ShapeDtypeStruct(q.shape, q.dtype)
    short_out = jax.ShapeDtypeStruct(qs.shape, qs.dtype)
    shapes = (long_out,) * 3 + (short_out,) * 3 + (jax.ShapeDtypeStruct(table.shape, F32),)
    results = pl.pallas_call(
        functools.partial(kernel, dp_size),
        out_shape=shapes,
        in_specs=[hbm] * 5 + [smem, vmem] + [hbm] * 5 + [smem, vmem, vmem],
        out_specs=(hbm,) * 6 + (vmem,),
        scratch_shapes=[pltpu.VMEM((7 * span, wide), BF16)] * 4
        + [pltpu.VMEM((span, width), BF16)] * 2
        + [pltpu.VMEM((4, 8, 128), F32), pltpu.VMEM((3, 8, 128), F32), pltpu.VMEM((3, 8, 128), F32)]
        + [pltpu.VMEM((rows, width), BF16)] * 8
        + [pltpu.VMEM((4 * span, wide), BF16)] * 3
        + [pltpu.VMEM((7 * span, wide), F32), pltpu.VMEM((2, 7 * span, 4 * span), F32)]
        + [pltpu.VMEM((2, 4 * span, 7 * span), BF16), pltpu.VMEM((2, 7 * span, 7 * span), BF16)]
        + [pltpu.VMEM((8, 128), F32), pltpu.VMEM((128, 128), F32), pltpu.VMEM((2, 16, 8, 128), F32)]
        + [
            dma((11,)), dma((4, 4)), dma((4, 4)), dma((3,)), dma((3,)), dma((4, 3)), dma((4, 3)),
            dma((3,)), dma((3,)), dma((3, 4)), dma((3, 4)), dma((3,)), dma((2, 15)), dma((2, 15)), dma((3,)),
        ],
        compiler_params=pltpu.CompilerParams(
            collective_id=0, has_side_effects=True, vmem_limit_bytes=VMEM_LIMIT
        ),
        name="window_grads",
    )(q, k, v, o, g, groups, gap_long, qs, ks, vs, os, gs, lengths, gap_short.reshape(1, -1), table)
    return pl.pallas_call(
        place_kernel,
        out_shape=shapes,
        in_specs=[hbm] * 7,
        out_specs=(hbm,) * 7,
        scratch_shapes=[pltpu.VMEM(shape.shape, shape.dtype) for shape in shapes] + [dma((7,)), dma((7,))],
        compiler_params=pltpu.CompilerParams(vmem_limit_bytes=VMEM_LIMIT),
        name="place",
    )(*results)


def solution(mesh):
    placed = (
        (P("dp", "blk", None),) * 5
        + (P("dp", None), P("dp", None))
        + (P(("dp", "blk"), None),) * 5
        + (P(("dp", "blk")), P(("dp", "blk")), P())
    )
    return jax.shard_map(
        functools.partial(body, mesh.shape["dp"]),
        mesh=mesh,
        in_specs=placed,
        out_specs=(P("dp", "blk", None),) * 3 + (P(("dp", "blk"), None),) * 3 + (P(),),
        check_vma=False,
    )
```
